256 devices in a mesh: crow: 16 (over y, z_lo, core), ccol: 16 (over z_hi, x).
Axes of the slice: x: 4, y: 4, z: 8 (z_hi: 4, z_lo: 2; z = z_hi * 2 + z_lo), core: 2. Of those that a mesh axis runs over, the one named last changes fastest.
Arguments:
- grad_rows: bfloat16 [2048, 16384], P('crow', 'ccol'), may hold values from -18 to 18
- labels: int32 [2048], replicated, may hold values from 0 to 16383
- class_weights: int32 [16384], P(('crow', 'ccol')), may hold values from 1 to 1024
- factor_old: float32 [16384, 16384], P('crow', 'ccol'), may hold values from -3 to 3
- inverse_old: bfloat16 [16384, 16384], P('crow', 'ccol'), may hold values from -0.046875 to 0.046875
- head_grad: bfloat16 [16384, 1280], P('ccol', 'crow'), may hold values from -6 to 6
Outputs:
- factor_new: float32 [16384, 16384], P('crow', 'ccol')
- preconditioned: bfloat16 [16384, 1280], P(('crow', 'ccol'))
The draws below stay inside these ranges and needn't reach their ends.
All inputs are finite; a program needn't handle non-finite values.
Results may differ from the reference program's by a relative error of at most 0.0021.
Values may be sent and summed in bfloat16 or wider, within the bound.
A program may use at most 128 MiB of HBM per device.

```python
import jax
import jax.numpy as jnp
from jax import lax

C = 16384
D = 1280
R = 2048
N_CROW = 16


def place_ends(drawn, rng, least, high):
    shape = drawn.shape
    index_at = [jax.random.randint(jax.random.fold_in(rng, axis), (), 0, shape[axis]) for axis in range(len(shape))]
    drawn = drawn.at[tuple(index_at)].set(least)
    longest = shape.index(max(shape))
    index_at[longest] = (index_at[longest] + 1) % shape[longest]
    return drawn.at[tuple(index_at)].set(high)


def level_of(stream_key, dims, split, smallest, high):
    factor_of, own = 1.0, jax.random.fold_in(stream_key, 6)
    for position, shards_of in split:
        steps = jnp.exp(jax.random.uniform(jax.random.fold_in(own, position), (shards_of,), jnp.float32, smallest / len(split), high / len(split)))
        factor_of = factor_of * jnp.repeat(steps, dims[position] // shards_of).reshape([-1 if axis == position else 1 for axis in range(len(dims))])
    return factor_of


def centred(stream_key, extent, scale, most, cuts=(), held_as=jnp.bfloat16):
    values = jax.random.normal(stream_key, extent, jnp.float32) * scale
    if len(cuts) > 0:
        values = level_of(stream_key, extent, cuts, -0.22, 0.18) * values
    return jnp.clip(values, min=-most, max=most).astype(held_as)


def setup_inputs(seed: int = 0) -> dict:
    arg_keys = jax.random.split(jax.random.key(seed), 7)
    grad_rows = centred(arg_keys[0], (R, C), 3.0, 18.0, ((0, 16), (1, 16)))
    labels = place_ends(jax.random.randint(arg_keys[1], (R,), 0, C), jax.random.fold_in(arg_keys[1], 1), 0, C - 1).astype(jnp.int32)
    class_weights = place_ends(jax.random.randint(arg_keys[2], (C,), 1, 1025), jax.random.fold_in(arg_keys[2], 1), 1, 1024).astype(jnp.int32)
    factor_old = centred(arg_keys[3], (C, C), 0.5, 3.0, ((0, 16), (1, 16)), jnp.float32)
    inverse_old = centred(arg_keys[4], (C, C), C ** -0.5, 0.046875, ((0, 16), (1, 16)))
    head_grad = centred(arg_keys[5], (C, D), 1.0, 6.0, ((0, 16), (1, 16)))
    return {"grad_rows": grad_rows, "labels": labels, "class_weights": class_weights, "factor_old": factor_old, "inverse_old": inverse_old, "head_grad": head_grad}


stat_decay = 0.75
weight_unit = 1024.0


def reference(grad_rows, labels, class_weights, factor_old, inverse_old, head_grad):
    row_weight = class_weights[labels].astype(jnp.float32) / weight_unit
    weight_sum = jnp.sum(row_weight)
    weighted = (row_weight[:, None] * grad_rows.astype(jnp.float32)).astype(jnp.bfloat16)
    tile_rows = C // N_CROW
    old_blocks = factor_old.reshape(N_CROW, tile_rows, C)
    grad_blocks = jnp.transpose(grad_rows.reshape(R, N_CROW, tile_rows), (1, 0, 2))

    def refresh(operands):
        old_block, grad_block = operands
        gram_tile = jnp.dot(grad_block.T, weighted, preferred_element_type=jnp.float32)
        return stat_decay * old_block + (1.0 - stat_decay) * gram_tile / weight_sum

    factor_new = lax.map(refresh, (old_blocks, grad_blocks)).reshape(C, C)
    inverse_blocks = inverse_old.reshape(N_CROW, tile_rows, C)

    def precondition(inverse_block):
        return jnp.dot(inverse_block, head_grad, preferred_element_type=jnp.float32).astype(jnp.bfloat16)

    preconditioned = lax.map(precondition, inverse_blocks).reshape(C, D)
    return factor_new, preconditioned
```

```python
import jax
import jax.numpy as jnp
from jax import lax
from jax.sharding import PartitionSpec as P

stat_decay = 0.75
weight_unit = 1024.0


def body(grad_rows, labels, class_weights, factor_old, inverse_old, head_grad):
    n = lax.axis_size("crow")
    m = lax.axis_size("ccol")
    grad_block = lax.all_gather(head_grad, "crow", axis=1, tiled=True)
    partial_value = jnp.dot(inverse_old, grad_block, preferred_element_type=jnp.float32)
    parts = lax.all_to_all(
        partial_value.reshape(m, -1, partial_value.shape[1]), "ccol", split_axis=0, concat_axis=0
    )
    preconditioned = jnp.sum(parts, axis=0).astype(jnp.bfloat16)
    class_table = lax.all_gather(class_weights, ("crow", "ccol"), axis=0, tiled=True)
    row_weight = class_table[labels].astype(jnp.float32) / weight_unit
    weight_sum = jnp.sum(row_weight)
    columns = lax.all_gather(grad_rows, "crow", axis=0, tiled=True)
    swapped = lax.ppermute(
        grad_rows, ("crow", "ccol"), [(r * m + c, c * m + r) for r in range(n) for c in range(m)]
    )
    pieces = lax.all_gather(swapped, "ccol", axis=0, tiled=True)
    weighted = (row_weight[:, None] * columns.astype(jnp.float32)).astype(jnp.bfloat16)
    gram_tile = lax.dot_general(
        pieces, weighted, (((0,), (0,)), ((), ())), preferred_element_type=jnp.float32
    )
    factor_new = stat_decay * factor_old + (1.0 - stat_decay) * gram_tile / weight_sum
    return (factor_new, preconditioned)


def solution(mesh):
    placed = (
        P("crow", "ccol"),
        P(),
        P(("crow", "ccol")),
        P("crow", "ccol"),
        P("crow", "ccol"),
        P("ccol", "crow"),
    )
    return jax.shard_map(
        body,
        mesh=mesh,
        in_specs=placed,
        out_specs=(P("crow", "ccol"), P(("crow", "ccol"), None)),
        check_vma=False,
    )
```

```python
import jax
import jax.numpy as jnp
from jax import lax
from jax.experimental import pallas as pl
from jax.experimental.pallas import tpu as pltpu
from jax.sharding import PartitionSpec as P

stat_decay = 0.75
weight_unit = 1024.0
MESH = pl.DeviceIdType.MESH
f32, bf16, i32, i16 = jnp.float32, jnp.bfloat16, jnp.int32, jnp.int16
top = 32767.0


def kernel(
    g_ref, head_ref, lab_ref, cw_ref, fold_in, inv_in,
    fout, pre_ref,
    g_t, head_t, hall, call, pall, wt, inv, fold, part, total,
    qxs, qxr, sxs, sxr, qzs, qzr, szs, szr,
    row, tab1, tabc, tab2,
    h_send, h_recv, g_send, g_recv, p_send, p_recv, w_send, w1_recv, w2_recv,
    x_send, xq_recv, xs_recv, z_send, zq_recv, zs_recv, loc,
):
    r, c = lax.axis_index("crow"), lax.axis_index("ccol")
    y, zl, k = r // 4, (r // 2) % 2, r % 2
    zh, x = c // 4, c % 4
    rid = lambda y, zl, k: lax.rem(y + 8, 4) * 4 + zl * 2 + k
    cid = lambda zh, x: lax.rem(zh + 8, 4) * 4 + lax.rem(x + 8, 4)
    y_right, y_left = (rid(y + 1, zl, k), c), (rid(y - 1, zl, k), c)
    pair, sibling = (rid(y, 1 - zl, k), c), (rid(y, zl, 1 - k), c)
    x_right, x_left = (r, cid(zh, x + 1)), (r, cid(zh, x - 1))
    z_right, z_left = (r, cid(zh + 1, x)), (r, cid(zh - 1, x))
    diagonal = r == c

    barrier = pltpu.get_barrier_semaphore()

    def greet(i, _):
        pl.semaphore_signal(barrier, inc=1, device_id=(lax.rem(r + i, 16), c), device_id_type=MESH)
        pl.semaphore_signal(barrier, inc=1, device_id=(r, lax.rem(c + i, 16)), device_id_type=MESH)
        return 0

    lax.fori_loop(1, 16, greet, 0)

    @pl.when(jnp.logical_not(diagonal))
    def _():
        pl.semaphore_signal(barrier, inc=1, device_id=(c, r), device_id_type=MESH)

    loads = []
    for d in range(4):
        for zo in range(4):
            owner = zo * 4 + lax.rem(x + d, 4)
            loads.append(
                pltpu.make_async_copy(
                    inv_in.at[pl.ds(pl.multiple_of(owner * 64, 64), 64)],
                    inv.at[d, pl.ds(zo * 64, 64)],
                    loc.at[d],
                )
            )
    for load in loads:
        load.start()
    fold_load = pltpu.make_async_copy(fold_in, fold, loc.at[4])
    fold_load.start()

    for j in range(8):
        g_t[j * 128 : (j + 1) * 128, :] = g_ref[:, j * 128 : (j + 1) * 128].T
        head_t[:, j * 128 : (j + 1) * 128] = head_ref[j * 128 : (j + 1) * 128, :].T
    row[...] = jnp.zeros_like(row)
    row[:, 0:64] = jnp.broadcast_to(cw_ref[...].astype(f32), (8, 64))
    tab1[r] = row[...]

    pl.semaphore_wait(barrier, jnp.where(diagonal, 30, 31))

    sent = []

    def send(src, dst, ssem, rsem, device):
        copy = pltpu.make_async_remote_copy(
            src_ref=src, dst_ref=dst, send_sem=ssem, recv_sem=rsem, device_id=device, device_id_type=MESH
        )
        copy.start()
        sent.append(copy)

    def landed(dst, rsem):
        pltpu.make_async_copy(dst, dst, rsem).wait()

    p_half = lambda slot, h: pall.at[slot, pl.ds(h * 512, 512)]

    def swap(h):
        return pltpu.make_async_remote_copy(
            src_ref=g_t.at[pl.ds(h * 512, 512)], dst_ref=p_half(r, h), send_sem=p_send,
            recv_sem=p_recv.at[r, h], device_id=(c, r), device_id_type=MESH,
        )

    @pl.when(jnp.logical_not(diagonal))
    def _():
        swap(0).start()
        swap(1).start()

    @pl.when(diagonal)
    def _():
        for h in range(2):
            pltpu.make_async_copy(g_t.at[pl.ds(h * 512, 512)], p_half(c, h), p_recv.at[c, h]).start()

    class Crow:
        def __init__(self, own, buf, depth, cut, ssem, rsem):
            self.own, self.buf, self.depth, self.cut = own, buf, depth, cut
            self.ssem, self.rsem = ssem, rsem

        def rows(self, h):
            return (0, self.cut) if h == 0 else (self.cut, self.depth - self.cut)

        def at(self, slot, h):
            start, size = self.rows(h)
            return self.buf.at[pl.ds(pl.multiple_of(slot * self.depth + start, 16), size)]

        def push(self, slot, h, device, own=False):
            start, size = self.rows(h)
            src = self.own.at[pl.ds(start, size)] if own else self.at(slot, h)
            send(src, self.at(slot, h), self.ssem, self.rsem.at[slot, h], device)

        def got(self, slot, h):
            landed(self.at(slot, h), self.rsem.at[slot, h])

        def start_pair(self):
            for h in (0, 1):
                self.push(r, h, pair, own=True)

        def start_ring(self):
            for h in (0, 1):
                self.push(r, h, y_right, own=True)
                self.push(r, 1 - h, y_left, own=True)

        def start_sibling(self):
            for h in (0, 1):
                self.push(r, h, sibling, own=True)

        def pass_pair(self):
            slot = rid(y, 1 - zl, k)
            for h in (0, 1):
                self.got(slot, h)
            for h in (0, 1):
                self.push(slot, h, y_right)
                self.push(slot, 1 - h, y_left)
            for h in (0, 1):
                self.push(slot, h, sibling)

        def pass_ring(self, zl):
            a, b = rid(y - 1, zl, k), rid(y + 1, zl, k)
            self.got(a, 0)
            self.push(a, 0, y_right)
            self.got(b, 1)
            self.push(b, 1, y_left)
            self.push(a, 0, sibling)
            self.push(b, 1, sibling)
            self.got(a, 1)
            self.push(a, 1, sibling)
            self.got(b, 0)
            self.push(b, 0, sibling)

        def end_ring(self, zl):
            a = rid(y + 2, zl, k)
            for h in (0, 1):
                self.got(a, h)
                self.push(a, h, sibling)

        def end(self):
            for dy in range(4):
                for z in (0, 1):
                    for h in (0, 1):
                        self.got(rid(y + dy, z, 1 - k), h)
            start = pl.multiple_of(r * self.depth, 16)
            self.buf[pl.ds(start, self.depth), :] = self.own[...]

    heads = Crow(head_t, hall, 80, 48, h_send, h_recv)
    grads = Crow(g_ref, call, 128, 64, g_send, g_recv)

    heads.start_pair()
    heads.start_ring()
    heads.start_sibling()

    def weights_out(i, _):
        pltpu.make_async_remote_copy(
            src_ref=row, dst_ref=tab1.at[r], send_sem=w_send, recv_sem=w1_recv.at[r],
            device_id=(lax.rem(r + i, 16), c), device_id_type=MESH,
        ).start()
        return 0

    lax.fori_loop(1, 16, weights_out, 0)

    grads.start_pair()
    grads.start_sibling()
    heads.pass_pair()
    heads.pass_ring(zl)
    heads.pass_ring(1 - zl)
    grads.start_ring()
    grads.pass_pair()
    heads.end_ring(zl)
    heads.end_ring(1 - zl)
    heads.end()

    def products(d):
        def tile(j, _):
            cols = pl.ds(pl.multiple_of(j * 256, 256), 256)
            part[d, :, cols] = lax.dot_general(
                inv[d], hall[cols, :], (((1,), (1,)), ((), ())), preferred_element_type=f32
            )
            return 0

        for load in loads[d * 4 : d * 4 + 4]:
            load.wait()
        lax.fori_loop(0, 5, tile, 0)

    class Reduce:
        def __init__(self, term, rows, left, right, qs, qr, ss, sr, ssem, qsem, usem):
            self.term, self.rows, self.to = term, rows, (left, right)
            self.qs, self.qr, self.ss, self.sr = qs, qr, ss, sr
            self.ssem, self.qsem, self.usem = ssem, qsem, usem

        def push(self, way, m, value):
            most = jnp.maximum(jnp.max(jnp.abs(value)), 1e-30)
            self.qs[way, m] = jnp.round(value * (top / most)).astype(i32).astype(i16)
            self.ss[way, m] = jnp.full((8, 128), most / top, f32)
            for src, dst, sem in ((self.qs, self.qr, self.qsem), (self.ss, self.sr, self.usem)):
                send(src.at[way, m], dst.at[way, m], self.ssem, sem.at[way, m], self.to[way])

        def pull(self, way, m):
            landed(self.qr.at[way, m], self.qsem.at[way, m])
            landed(self.sr.at[way, m], self.usem.at[way, m])
            unit = self.sr[way, m][0:1, 0:1]
            return self.qr[way, m].astype(i32).astype(f32) * unit

        def first(self):
            self.push(0, 0, self.term(2, 0))
            self.push(1, 0, self.term(2, 1))

        def second(self):
            self.push(0, 1, self.term(3, 1))
            self.push(1, 1, self.term(1, 0))

        def third(self):
            self.push(0, 2, self.term(3, 0) + self.pull(0, 0))
            self.push(1, 2, self.term(1, 1) + self.pull(1, 0))

        def last(self, p):
            own = self.term(0, p)
            return own + self.pull(0, 2 if p == 0 else 1) + self.pull(1, 1 if p == 0 else 2)

    over_x = Reduce(
        lambda d, p: part[d, p * 128 : (p + 1) * 128, :], 128, x_left, x_right,
        qxs, qxr, sxs, sxr, x_send, xq_recv, xs_recv,
    )

    def z_term(d, p):
        start = lax.rem(zh + d, 4) * 64 + p * 32
        return total[pl.ds(pl.multiple_of(start, 32), 32), :]

    over_z = Reduce(z_term, 32, z_left, z_right, qzs, qzr, szs, szr, z_send, zq_recv, zs_recv)

    products(2)
    over_x.first()
    products(3)
    products(1)
    over_x.second()

    def p_push(slot, h, device):
        send(p_half(slot, h), p_half(slot, h), p_send, p_recv.at[slot, h], device)

    def p_got(slot, h):
        landed(p_half(slot, h), p_recv.at[slot, h])

    def x_out(slot, first):
        p_push(slot, first, x_right if first == 0 else x_left)
        p_push(slot, 1 - first, x_left if first == 0 else x_right)

    p_got(c, 0)
    p_got(c, 1)
    for h in (0, 1):
        p_push(c, h, z_right)
        p_push(c, 1 - h, z_left)
    for h in (0, 1):
        p_push(c, h, x_right)
        p_push(c, 1 - h, x_left)

    over_x.third()
    grads.pass_ring(zl)
    products(0)

    def z_pass():
        a, b = cid(zh - 1, x), cid(zh + 1, x)
        p_got(a, 0)
        p_push(a, 0, z_right)
        p_got(b, 1)
        p_push(b, 1, z_left)
        p_got(a, 1)
        for h in (0, 1):
            p_push(a, h, x_right)
            p_push(a, 1 - h, x_left)
        p_got(b, 0)
        for h in (0, 1):
            p_push(b, h, x_right)
            p_push(b, 1 - h, x_left)

    def x_pass(dz):
        a, b = cid(zh + dz, x - 1), cid(zh + dz, x + 1)
        p_got(a, 0)
        p_push(a, 0, x_right)
        p_got(b, 1)
        p_push(b, 1, x_left)

    def x_end(dz):
        a, b, o = cid(zh + dz, x - 1), cid(zh + dz, x + 1), cid(zh + dz, x + 2)
        p_got(a, 1)
        p_got(b, 0)
        p_got(o, 0)
        p_got(o, 1)

    z_pass()
    grads.pass_ring(1 - zl)
    x_pass(0)

    for p in (0, 1):
        total[p * 128 : (p + 1) * 128, :] = over_x.last(p)
    over_z.first()
    over_z.second()

    a = cid(zh + 2, x)
    for h in (0, 1):
        p_got(a, h)
        p_push(a, h, x_right)
        p_push(a, h, x_left)
    grads.end_ring(zl)
    grads.end_ring(1 - zl)
    x_pass(-1)
    over_z.third()

    def weights_in(i, _):
        slot = lax.rem(r + i, 16)
        landed(tab1.at[slot], w1_recv.at[slot])
        return 0

    lax.fori_loop(1, 16, weights_in, 0)
    tabc[...] = tab1[:, 0, :]
    tab2[c] = tabc[...]

    def weights_on(i, _):
        pltpu.make_async_remote_copy(
            src_ref=tabc, dst_ref=tab2.at[c], send_sem=w_send, recv_sem=w2_recv.at[c],
            device_id=(r, lax.rem(c + i, 16)), device_id_type=MESH,
        ).start()
        return 0

    lax.fori_loop(1, 16, weights_on, 0)
    x_pass(1)
    grads.end()
    for p in (0, 1):
        pre_ref[p * 32 : (p + 1) * 32, :] = over_z.last(p).astype(bf16)

    def weights_all(i, _):
        slot = lax.rem(c + i, 16)
        landed(tab2.at[slot], w2_recv.at[slot])
        return 0

    lax.fori_loop(1, 16, weights_all, 0)

    table = tab2[...].reshape(256, 128).astype(i32)
    table_hi = ((table >> 5) << 5).astype(f32).astype(bf16)
    table_lo = (table & 31).astype(f32).astype(bf16)
    lanes = lax.broadcasted_iota(i32, (128, 256), 1)
    lane = lax.broadcasted_iota(i32, (128, 128), 1)

    def weigh(b, weight_sum):
        lab = jnp.broadcast_to(lab_ref[pl.ds(b, 1), :].astype(f32), (128, 128)).T.astype(i32)
        at = ((lab >> 6) & 15) * 16 + (lab >> 10)
        hot = (lanes == jnp.concatenate([at, at], axis=1)).astype(f32).astype(bf16)
        picked = jnp.dot(hot, table_hi, preferred_element_type=f32)
        picked += jnp.dot(hot, table_lo, preferred_element_type=f32)
        weight = jnp.sum(jnp.where(lane == (lab & 63), picked, 0.0), axis=1, keepdims=True) / weight_unit
        rows = pl.ds(pl.multiple_of(b * 128, 128), 128)
        wt[rows, :] = (weight * call[rows, :].astype(f32)).astype(bf16)
        return weight_sum + jnp.sum(weight)

    weight_sum = lax.fori_loop(0, 16, weigh, jnp.float32(0.0))
    gram_unit = (1.0 - stat_decay) / weight_sum
    fold_load.wait()

    def gram(sets, i, j):
        value = None
        for dz in sets:
            first = lax.rem(zh + dz + 8, 4) * 4
            left = jnp.concatenate([pall[first + q, pl.ds(i * 512, 512), :] for q in range(4)], axis=1)
            right = wt[pl.ds(pl.multiple_of(first * 128, 512), 512), pl.ds(pl.multiple_of(j * 256, 256), 256)]
            term = jnp.dot(left, right, preferred_element_type=f32)
            value = term if value is None else value + term
        return value

    def gram_early(j, _):
        cols = pl.ds(pl.multiple_of(j * 256, 256), 256)
        for i in range(2):
            rows = pl.ds(i * 512, 512)
            fold[rows, cols] = stat_decay * fold[rows, cols] + gram_unit * gram((0, -1, 1), i, j)
        return 0

    x_pass(2)
    x_end(0)
    x_end(-1)
    x_end(1)
    lax.fori_loop(0, 4, gram_early, 0)
    x_end(2)
    stores = []
    for i in range(2):
        rows = pl.ds(i * 512, 512)

        def gram_late(j, _):
            cols = pl.ds(pl.multiple_of(j * 256, 256), 256)
            fold[rows, cols] += gram_unit * gram((2,), i, j)
            return 0

        lax.fori_loop(0, 4, gram_late, 0)
        store = pltpu.make_async_copy(fold.at[rows], fout.at[rows], loc.at[5 + i])
        store.start()
        stores.append(store)

    for copy in sent:
        copy.wait_send()

    @pl.when(jnp.logical_not(diagonal))
    def _():
        swap(0).wait_send()
        swap(1).wait_send()

    def weights_left(i, _):
        pltpu.make_async_remote_copy(
            src_ref=row, dst_ref=tab1.at[r], send_sem=w_send, recv_sem=w1_recv.at[r],
            device_id=(lax.rem(r + i, 16), c), device_id_type=MESH,
        ).wait_send()
        pltpu.make_async_remote_copy(
            src_ref=tabc, dst_ref=tab2.at[c], send_sem=w_send, recv_sem=w2_recv.at[c],
            device_id=(r, lax.rem(c + i, 16)), device_id_type=MESH,
        ).wait_send()
        return 0

    lax.fori_loop(1, 16, weights_left, 0)
    for store in stores:
        store.wait()


def body(grad_rows, labels, class_weights, factor_old, inverse_old, head_grad):
    vmem, anywhere = pl.BlockSpec(memory_space=pltpu.VMEM), pl.BlockSpec(memory_space=pl.ANY)
    dma = pltpu.SemaphoreType.DMA
    factor_new, preconditioned = pl.pallas_call(
        kernel,
        out_shape=(
            jax.ShapeDtypeStruct((1024, 1024), f32),
            jax.ShapeDtypeStruct((64, 1280), bf16),
        ),
        in_specs=[vmem, vmem, vmem, vmem, anywhere, anywhere],
        out_specs=(anywhere, vmem),
        scratch_shapes=[
            pltpu.VMEM((1024, 128), bf16),
            pltpu.VMEM((80, 1024), bf16),
            pltpu.VMEM((1280, 1024), bf16),
            pltpu.VMEM((2048, 1024), bf16),
            pltpu.VMEM((16, 1024, 128), bf16),
            pltpu.VMEM((2048, 1024), bf16),
            pltpu.VMEM((4, 256, 1024), bf16),
            pltpu.VMEM((1024, 1024), f32),
            pltpu.VMEM((4, 256, 1280), f32),
            pltpu.VMEM((256, 1280), f32),
            pltpu.VMEM((2, 3, 128, 1280), i16),
            pltpu.VMEM((2, 3, 128, 1280), i16),
            pltpu.VMEM((2, 3, 8, 128), f32),
            pltpu.VMEM((2, 3, 8, 128), f32),
            pltpu.VMEM((2, 3, 32, 1280), i16),
            pltpu.VMEM((2, 3, 32, 1280), i16),
            pltpu.VMEM((2, 3, 8, 128), f32),
            pltpu.VMEM((2, 3, 8, 128), f32),
            pltpu.VMEM((8, 128), f32),
            pltpu.VMEM((16, 8, 128), f32),
            pltpu.VMEM((16, 128), f32),
            pltpu.VMEM((16, 16, 128), f32),
                dma, dma((16, 2)), dma, dma((16, 2)), dma, dma((16, 2)),
            dma, dma((16,)), dma((16,)),
            dma, dma((2, 3)), dma((2, 3)), dma, dma((2, 3)), dma((2, 3)),
            dma((7,)),
        ],
        compiler_params=pltpu.CompilerParams(
            collective_id=0, has_side_effects=True, vmem_limit_bytes=58 << 20
        ),
        name="kfac",
    )(
        grad_rows,
        head_grad,
        labels.reshape(16, 128),
        class_weights.reshape(1, 64),
        factor_old,
        inverse_old,
    )
    return factor_new, preconditioned


def solution(mesh):
    placed = (
        P("crow", "ccol"),
        P(),
        P(("crow", "ccol")),
        P("crow", "ccol"),
        P("crow", "ccol"),
        P("ccol", "crow"),
    )
    return jax.shard_map(
        body,
        mesh=mesh,
        in_specs=placed,
        out_specs=(P("crow", "ccol"), P(("crow", "ccol"), None)),
        check_vma=False,
    )
```

```python
import jax
import jax.numpy as jnp
from jax import lax
from jax.experimental import pallas as pl
from jax.experimental.pallas import tpu as pltpu
from jax.sharding import PartitionSpec as P

stat_decay = 0.75
weight_unit = 1024.0
MESH = pl.DeviceIdType.MESH
f32, bf16, i32, i16 = jnp.float32, jnp.bfloat16, jnp.int32, jnp.int16
top = 32767.0
split = 768


def kernel(
    g_ref, head_t, lab_ref, cw_ref, fold_in, inv_in,
    fout, pre_ref,
    g_t, t_mid, hall, call, pall, wt, inv, fold, part_x, total_z, part_z, total_x,
    *rest,
):
    moves, rest = [rest[i * 7 : i * 7 + 7] for i in range(4)], rest[28:]
    row, tab1, tabc, tab2, h_send, h_recv, g_send, g_recv, p_send, p_recv, *rest = rest
    t_send, t_recv, w_send, w1_recv, w2_recv, loc = rest
    r, c = lax.axis_index("crow"), lax.axis_index("ccol")
    y, zl, k = r // 4, (r // 2) % 2, r % 2
    zh, x = c // 4, c % 4
    rid = lambda y, zl, k: lax.rem(y + 8, 4) * 4 + zl * 2 + k
    cid = lambda zh, x: lax.rem(zh + 8, 4) * 4 + lax.rem(x + 8, 4)
    y_right, y_left = (rid(y + 1, zl, k), c), (rid(y - 1, zl, k), c)
    pair, sibling = (rid(y, 1 - zl, k), c), (rid(y, zl, 1 - k), c)
    wrap = lambda v: lax.rem(v + 8, 4)
    x_right, x_left = (r, cid(zh, x + 1)), (r, cid(zh, x - 1))
    z_right, z_left = (r, cid(zh + 1, x)), (r, cid(zh - 1, x))

    mine = 2 * zl + k
    t1_to = (rid(y, x // 2, lax.rem(x, 2)), cid(zh + mine, x + zh + y))
    far = wrap(x - mine - y)
    off = wrap(zh - far)
    t1_from = (rid(y, off // 2, lax.rem(off, 2)), far * 4 + mine)
    t1_stays = (t1_to[0] == r) & (t1_to[1] == c)
    t2_to = (rid(far, zl, k), c)
    t2_stays = far == y

    barrier = pltpu.get_barrier_semaphore()

    def greet(i, _):
        pl.semaphore_signal(barrier, inc=1, device_id=(lax.rem(r + i, 16), c), device_id_type=MESH)
        pl.semaphore_signal(barrier, inc=1, device_id=(r, lax.rem(c + i, 16)), device_id_type=MESH)
        return 0

    lax.fori_loop(1, 16, greet, 0)

    @pl.when(jnp.logical_not(t1_stays))
    def _():
        pl.semaphore_signal(barrier, inc=1, device_id=t1_to, device_id_type=MESH)
        pl.semaphore_signal(barrier, inc=1, device_id=t1_from, device_id_type=MESH)

    loads = []
    for d in range(4):
        for zo in range(4):
            owner = zo * 4 + lax.rem(x + d, 4)
            loads.append(
                pltpu.make_async_copy(
                    inv_in.at[pl.ds(pl.multiple_of(owner * 64, 64), 64)],
                    inv.at[d, pl.ds(zo * 64, 64)],
                    loc.at[d],
                )
            )
    for load in loads:
        load.start()
    fold_load = pltpu.make_async_copy(fold_in, fold, loc.at[4])
    fold_load.start()

    for j in range(8):
        g_t[j * 128 : (j + 1) * 128, :] = g_ref[:, j * 128 : (j + 1) * 128].T
    row[...] = jnp.zeros_like(row)
    row[:, 0:64] = jnp.broadcast_to(cw_ref[...].astype(f32), (8, 64))
    tab1[r] = row[...]

    pl.semaphore_wait(barrier, jnp.where(t1_stays, 30, 32))

    sent = []

    def send(src, dst, ssem, rsem, device):
        copy = pltpu.make_async_remote_copy(
            src_ref=src, dst_ref=dst, send_sem=ssem, recv_sem=rsem, device_id=device, device_id_type=MESH
        )
        copy.start()
        sent.append(copy)

    def landed(dst, rsem):
        pltpu.make_async_copy(dst, dst, rsem).wait()

    half = lambda ref, h: ref.at[pl.ds(h * 512, 512)]
    p_half = lambda slot, h: pall.at[slot, pl.ds(h * 512, 512)]

    def step(h, src, dst, ssem, rsem, device):
        return pltpu.make_async_remote_copy(
            src_ref=src, dst_ref=dst, send_sem=ssem, recv_sem=rsem, device_id=device, device_id_type=MESH
        )

    t1 = lambda h: step(h, half(g_t, h), half(t_mid, h), t_send.at[0], t_recv.at[h], t1_to)
    t2 = lambda h: step(h, half(t_mid, h), p_half(c, h), t_send.at[1], p_recv.at[c, h], t2_to)

    @pl.when(jnp.logical_not(t1_stays))
    def _():
        t1(0).start()
        t1(1).start()

    @pl.when(t1_stays)
    def _():
        for h in range(2):
            pltpu.make_async_copy(half(g_t, h), half(t_mid, h), t_recv.at[h]).start()

    def t_pass():
        for h in range(2):
            landed(half(t_mid, h), t_recv.at[h])

            @pl.when(jnp.logical_not(t2_stays))
            def _():
                t2(h).start()

            @pl.when(t2_stays)
            def _():
                pltpu.make_async_copy(half(t_mid, h), p_half(c, h), p_recv.at[c, h]).start()

    class Crow:
        def __init__(self, own, buf, depth, cut, ssem, rsem):
            self.own, self.buf, self.depth, self.cut = own, buf, depth, cut
            self.ssem, self.rsem = ssem, rsem

        def rows(self, h):
            return (0, self.cut) if h == 0 else (self.cut, self.depth - self.cut)

        def at(self, slot, h):
            start, size = self.rows(h)
            return self.buf.at[pl.ds(pl.multiple_of(slot * self.depth + start, 16), size)]

        def push(self, slot, h, device, own=False):
            start, size = self.rows(h)
            src = self.own.at[pl.ds(start, size)] if own else self.at(slot, h)
            send(src, self.at(slot, h), self.ssem, self.rsem.at[slot, h], device)

        def got(self, slot, h):
            landed(self.at(slot, h), self.rsem.at[slot, h])

        def start_pair(self):
            for h in (0, 1):
                self.push(r, h, pair, own=True)

        def start_ring(self):
            for h in (0, 1):
                self.push(r, h, y_right, own=True)
                self.push(r, 1 - h, y_left, own=True)

        def start_sibling(self):
            for h in (0, 1):
                self.push(r, h, sibling, own=True)

        def pass_pair(self):
            slot = rid(y, 1 - zl, k)
            for h in (0, 1):
                self.got(slot, h)
            for h in (0, 1):
                self.push(slot, h, y_right)
                self.push(slot, 1 - h, y_left)
            for h in (0, 1):
                self.push(slot, h, sibling)

        def pass_ring(self, zl):
            a, b = rid(y - 1, zl, k), rid(y + 1, zl, k)
            self.got(a, 0)
            self.push(a, 0, y_right)
            self.got(b, 1)
            self.push(b, 1, y_left)
            self.push(a, 0, sibling)
            self.push(b, 1, sibling)
            self.got(a, 1)
            self.push(a, 1, sibling)
            self.got(b, 0)
            self.push(b, 0, sibling)

        def end_ring(self, zl):
            a = rid(y + 2, zl, k)
            for h in (0, 1):
                self.got(a, h)
                self.push(a, h, sibling)

        def end(self):
            for dy in range(4):
                for z in (0, 1):
                    for h in (0, 1):
                        self.got(rid(y + dy, z, 1 - k), h)
            start = pl.multiple_of(r * self.depth, 16)
            self.buf[pl.ds(start, self.depth), :] = self.own[...]

    heads = Crow(head_t, hall, 80, 48, h_send, h_recv)
    grads = Crow(g_ref, call, 128, 64, g_send, g_recv)

    def weights_out(i, _):
        pltpu.make_async_remote_copy(
            src_ref=row, dst_ref=tab1.at[r], send_sem=w_send, recv_sem=w1_recv.at[r],
            device_id=(lax.rem(r + i, 16), c), device_id_type=MESH,
        ).start()
        return 0

    def p_push(slot, h, device):
        send(p_half(slot, h), p_half(slot, h), p_send, p_recv.at[slot, h], device)

    def p_got(slot, h):
        landed(p_half(slot, h), p_recv.at[slot, h])

    def p_start():
        p_got(c, 0)
        p_got(c, 1)
        for h in (0, 1):
            p_push(c, h, z_right)
            p_push(c, 1 - h, z_left)
        for h in (0, 1):
            p_push(c, h, x_right)
            p_push(c, 1 - h, x_left)

    def z_pass():
        a, b = cid(zh - 1, x), cid(zh + 1, x)
        p_got(a, 0)
        p_push(a, 0, z_right)
        p_got(b, 1)
        p_push(b, 1, z_left)
        p_got(a, 1)
        for h in (0, 1):
            p_push(a, h, x_right)
            p_push(a, 1 - h, x_left)
        p_got(b, 0)
        for h in (0, 1):
            p_push(b, h, x_right)
            p_push(b, 1 - h, x_left)

    def x_pass(dz):
        a, b = cid(zh + dz, x - 1), cid(zh + dz, x + 1)
        p_got(a, 0)
        p_push(a, 0, x_right)
        p_got(b, 1)
        p_push(b, 1, x_left)

    def x_end(dz):
        a, b, o = cid(zh + dz, x - 1), cid(zh + dz, x + 1), cid(zh + dz, x + 2)
        p_got(a, 1)
        p_got(b, 0)
        p_got(o, 0)
        p_got(o, 1)

    def z_end():
        a = cid(zh + 2, x)
        for h in (0, 1):
            p_got(a, h)
            p_push(a, h, x_right)
            p_push(a, h, x_left)

    def dot_heads(left, cols):
        return lax.dot_general(left, hall[cols, :], (((1,), (1,)), ((), ())), preferred_element_type=f32)

    def products_x(d):
        def tile(j, _):
            cols = pl.ds(pl.multiple_of(j * 256, 256), 256)
            part_x[d, :, cols] = dot_heads(inv[d], cols)
            return 0

        lax.fori_loop(0, split // 256, tile, 0)

    def products_z(d):
        rows = pl.ds(pl.multiple_of(lax.rem(zh + d, 4) * 64, 64), 64)
        left = jnp.concatenate([inv[dx, rows, :] for dx in range(4)], axis=0)

        def tile(j, _):
            cols = pl.ds(pl.multiple_of(j * 256, 256), 256)
            part_z[d, :, cols] = dot_heads(left, pl.ds(pl.multiple_of(split + j * 256, 256), 256))
            return 0

        lax.fori_loop(0, (1280 - split) // 256, tile, 0)

    class Reduce:
        def __init__(self, term, left, right, qs, qr, ss, sr, ssem, qsem, usem):
            self.term, self.to = term, (left, right)
            self.qs, self.qr, self.ss, self.sr = qs, qr, ss, sr
            self.ssem, self.qsem, self.usem = ssem, qsem, usem

        def push(self, way, m, value):
            most = jnp.maximum(jnp.max(jnp.abs(value)), 1e-30)
            self.qs[way, m] = jnp.round(value * (top / most)).astype(i32).astype(i16)
            self.ss[way, m] = jnp.full((8, 128), most / top, f32)
            for src, dst, sem in ((self.qs, self.qr, self.qsem), (self.ss, self.sr, self.usem)):
                send(src.at[way, m], dst.at[way, m], self.ssem, sem.at[way, m], self.to[way])

        def pull(self, way, m):
            landed(self.qr.at[way, m], self.qsem.at[way, m])
            landed(self.sr.at[way, m], self.usem.at[way, m])
            unit = self.sr[way, m][0:1, 0:1]
            return self.qr[way, m].astype(i32).astype(f32) * unit

        def first(self):
            self.push(0, 0, self.term(2, 0))
            self.push(1, 0, self.term(2, 1))

        def second(self):
            self.push(0, 1, self.term(3, 1))
            self.push(1, 1, self.term(1, 0))

        def third(self):
            self.push(0, 2, self.term(3, 0) + self.pull(0, 0))
            self.push(1, 2, self.term(1, 1) + self.pull(1, 0))

        def last(self, p):
            own = self.term(0, p)
            return own + self.pull(0, 2 if p == 0 else 1) + self.pull(1, 1 if p == 0 else 2)

        def total(self, ref):
            for p in (0, 1):
                ref[p * 128 : (p + 1) * 128, :] = self.last(p)

        def result(self, cols):
            for p in (0, 1):
                pre_ref[p * 32 : (p + 1) * 32, cols] = self.last(p).astype(bf16)

    def z_term(d, p):
        start = lax.rem(zh + d, 4) * 64 + p * 32
        return total_z[pl.ds(pl.multiple_of(start, 32), 32), :]

    x_first = Reduce(lambda d, p: part_x[d, p * 128 : (p + 1) * 128, :], x_left, x_right, *moves[0])
    then_z = Reduce(z_term, z_left, z_right, *moves[1])
    z_first = Reduce(lambda d, p: part_z[d, p * 128 : (p + 1) * 128, :], z_left, z_right, *moves[2])
    then_x = Reduce(lambda d, p: total_x[d * 64 + p * 32 : d * 64 + p * 32 + 32, :], x_left, x_right, *moves[3])

    def weights_in(i, _):
        slot = lax.rem(r + i, 16)
        landed(tab1.at[slot], w1_recv.at[slot])
        return 0

    def weights_on(i, _):
        pltpu.make_async_remote_copy(
            src_ref=tabc, dst_ref=tab2.at[c], send_sem=w_send, recv_sem=w2_recv.at[c],
            device_id=(r, lax.rem(c + i, 16)), device_id_type=MESH,
        ).start()
        return 0

    def weights_all(i, _):
        slot = lax.rem(c + i, 16)
        landed(tab2.at[slot], w2_recv.at[slot])
        return 0

    heads.start_ring()
    heads.start_pair()
    heads.start_sibling()
    lax.fori_loop(1, 16, weights_out, 0)
    heads.pass_pair()
    t_pass()
    heads.pass_ring(zl)
    grads.start_pair()
    grads.start_sibling()
    p_start()
    heads.pass_ring(1 - zl)
    grads.start_ring()
    grads.pass_pair()
    lax.fori_loop(1, 16, weights_in, 0)
    tabc[...] = tab1[:, 0, :]
    tab2[c] = tabc[...]
    lax.fori_loop(1, 16, weights_on, 0)
    heads.end_ring(zl)
    heads.end_ring(1 - zl)
    heads.end()
    for load in loads:
        load.wait()
    products_x(2)
    x_first.first()
    z_pass()
    products_z(2)
    z_first.first()
    products_x(3)
    products_x(1)
    x_first.second()
    products_z(3)
    products_z(1)
    z_first.second()
    grads.pass_ring(zl)
    x_pass(0)
    grads.pass_ring(1 - zl)
    x_first.third()
    z_end()
    products_x(0)
    products_z(0)
    grads.end_ring(zl)
    grads.end_ring(1 - zl)
    z_first.third()
    x_pass(-1)
    x_pass(1)
    grads.end()
    lax.fori_loop(1, 16, weights_all, 0)

    table = tab2[...].reshape(256, 128).astype(i32)
    table_hi = ((table >> 5) << 5).astype(f32).astype(bf16)
    table_lo = (table & 31).astype(f32).astype(bf16)
    lanes = lax.broadcasted_iota(i32, (128, 256), 1)
    lane = lax.broadcasted_iota(i32, (128, 128), 1)

    def weigh(b, weight_sum):
        held = wrap(lax.rem(b, 4) - mine - y) * 4 + wrap(b // 4 - y)
        lab = jnp.broadcast_to(lab_ref[pl.ds(held, 1), :].astype(f32), (128, 128)).T.astype(i32)
        at = ((lab >> 6) & 15) * 16 + (lab >> 10)
        hot = (lanes == jnp.concatenate([at, at], axis=1)).astype(f32).astype(bf16)
        picked = jnp.dot(hot, table_hi, preferred_element_type=f32)
        picked += jnp.dot(hot, table_lo, preferred_element_type=f32)
        weight = jnp.sum(jnp.where(lane == (lab & 63), picked, 0.0), axis=1, keepdims=True) / weight_unit
        rows = pl.ds(pl.multiple_of(held * 128, 128), 128)
        wt[pl.ds(pl.multiple_of(b * 128, 128), 128), :] = (weight * call[rows, :].astype(f32)).astype(bf16)
        return weight_sum + jnp.sum(weight)

    weight_sum = lax.fori_loop(0, 6, weigh, jnp.float32(0.0))
    x_first.total(total_z)
    then_z.first()
    then_z.second()
    weight_sum = lax.fori_loop(6, 11, weigh, weight_sum)
    z_first.total(total_x)
    then_x.first()
    then_x.second()
    x_pass(2)
    then_z.third()
    then_x.third()
    weight_sum = lax.fori_loop(11, 16, weigh, weight_sum)
    gram_unit = (1.0 - stat_decay) / weight_sum
    fold_load.wait()

    def gram(sets, i, j):
        value = None
        for dz in sets:
            first = lax.rem(zh + dz + 8, 4) * 4
            left = jnp.concatenate([pall[first + q, pl.ds(i * 512, 512), :] for q in range(4)], axis=1)
            right = wt[pl.ds(pl.multiple_of(first * 128, 512), 512), pl.ds(pl.multiple_of(j * 256, 256), 256)]
            term = jnp.dot(left, right, preferred_element_type=f32)
            value = term if value is None else value + term
        return value

    def gram_early(sets):
        def tile(j, _):
            cols = pl.ds(pl.multiple_of(j * 256, 256), 256)
            for i in range(2):
                rows = pl.ds(i * 512, 512)
                old = fold[rows, cols]
                if sets[0] == 0:
                    old = stat_decay * old
                fold[rows, cols] = old + gram_unit * gram(sets, i, j)
            return 0

        lax.fori_loop(0, 4, tile, 0)

    x_end(0)
    gram_early((0,))
    x_end(-1)
    gram_early((-1,))
    x_end(1)
    gram_early((1,))
    then_z.result(slice(0, split))
    then_x.result(slice(split, 1280))
    x_end(2)
    stores = []
    for i in range(2):
        rows = pl.ds(i * 512, 512)

        def gram_late(j, _):
            cols = pl.ds(pl.multiple_of(j * 256, 256), 256)
            fold[rows, cols] += gram_unit * gram((2,), i, j)
            return 0

        lax.fori_loop(0, 4, gram_late, 0)
        store = pltpu.make_async_copy(fold.at[rows], fout.at[rows], loc.at[5 + i])
        store.start()
        stores.append(store)

    for copy in sent:
        copy.wait_send()

    @pl.when(jnp.logical_not(t1_stays))
    def _():
        for h in range(2):
            t1(h).wait_send()

    @pl.when(jnp.logical_not(t2_stays))
    def _():
        for h in range(2):
            t2(h).wait_send()

    def weights_left(i, _):
        pltpu.make_async_remote_copy(
            src_ref=row, dst_ref=tab1.at[r], send_sem=w_send, recv_sem=w1_recv.at[r],
            device_id=(lax.rem(r + i, 16), c), device_id_type=MESH,
        ).wait_send()
        pltpu.make_async_remote_copy(
            src_ref=tabc, dst_ref=tab2.at[c], send_sem=w_send, recv_sem=w2_recv.at[c],
            device_id=(r, lax.rem(c + i, 16)), device_id_type=MESH,
        ).wait_send()
        return 0

    lax.fori_loop(1, 16, weights_left, 0)
    for store in stores:
        store.wait()


def messages(rows, columns):
    dma = pltpu.SemaphoreType.DMA
    return (
        *[pltpu.VMEM((2, 3, rows, columns), i16)] * 2,
        *[pltpu.VMEM((2, 3, 8, 128), f32)] * 2,
        dma,
        dma((2, 3)),
        dma((2, 3)),
    )


def body(grad_rows, labels, class_weights, factor_old, inverse_old, head_grad):
    vmem, anywhere = pl.BlockSpec(memory_space=pltpu.VMEM), pl.BlockSpec(memory_space=pl.ANY)
    dma = pltpu.SemaphoreType.DMA
    factor_new, preconditioned = pl.pallas_call(
        kernel,
        out_shape=(
            jax.ShapeDtypeStruct((1024, 1024), f32),
            jax.ShapeDtypeStruct((64, 1280), bf16),
        ),
        in_specs=[vmem, vmem, vmem, vmem, anywhere, anywhere],
        out_specs=(anywhere, vmem),
        scratch_shapes=[
            pltpu.VMEM((1024, 128), bf16),
            pltpu.VMEM((1024, 128), bf16),
            pltpu.VMEM((1280, 1024), bf16),
            pltpu.VMEM((2048, 1024), bf16),
            pltpu.VMEM((16, 1024, 128), bf16),
            pltpu.VMEM((2048, 1024), bf16),
            pltpu.VMEM((4, 256, 1024), bf16),
            pltpu.VMEM((1024, 1024), f32),
            pltpu.VMEM((4, 256, split), f32),
            pltpu.VMEM((256, split), f32),
            pltpu.VMEM((4, 256, 1280 - split), f32),
            pltpu.VMEM((256, 1280 - split), f32),
            *messages(128, split),
            *messages(32, split),
            *messages(128, 1280 - split),
            *messages(32, 1280 - split),
            pltpu.VMEM((8, 128), f32),
            pltpu.VMEM((16, 8, 128), f32),
            pltpu.VMEM((16, 128), f32),
            pltpu.VMEM((16, 16, 128), f32),
                dma, dma((16, 2)), dma, dma((16, 2)), dma, dma((16, 2)),
            dma((2,)), dma((2,)), dma, dma((16,)), dma((16,)),
            dma((7,)),
        ],
        compiler_params=pltpu.CompilerParams(
            collective_id=0, has_side_effects=True, vmem_limit_bytes=58 << 20
        ),
        name="kfac",
    )(
        grad_rows,
        head_grad.T,
        labels.reshape(16, 128),
        class_weights.reshape(1, 64),
        factor_old,
        inverse_old,
    )
    return factor_new, preconditioned


def solution(mesh):
    placed = (
        P("crow", "ccol"),
        P(),
        P(("crow", "ccol")),
        P("crow", "ccol"),
        P("crow", "ccol"),
        P("ccol", "crow"),
    )
    return jax.shard_map(
        body,
        mesh=mesh,
        in_specs=placed,
        out_specs=(P("crow", "ccol"), P(("crow", "ccol"), None)),
        check_vma=False,
    )
```

```python
import jax
import jax.numpy as jnp
from jax import lax
from jax.experimental import pallas as pl
from jax.experimental.pallas import tpu as pltpu
from jax.sharding import PartitionSpec as P

stat_decay = 0.75
weight_unit = 1024.0
MESH = pl.DeviceIdType.MESH
f32, bf16, i32, i16 = jnp.float32, jnp.bfloat16, jnp.int32, jnp.int16
top = 32767.0
split = 768


def kernel(
    g_ref, head_t, lab_ref, cw_ref, fold_in, inv_in,
    fout, pre_ref,
    g_t, t_mid, hall, call, pall, wt, inv, fold, part_x, total_z, part_z, total_x,
    *rest,
):
    moves, rest = [rest[i * 7 : i * 7 + 7] for i in range(4)], rest[28:]
    row, tab1, tabc, tab2, h_send, h_recv, g_send, g_recv, p_send, p_recv, *rest = rest
    t_send, t_recv, w_send, w1_recv, w2_recv, loc = rest
    r, c = lax.axis_index("crow"), lax.axis_index("ccol")
    y, zl, k = r // 4, (r // 2) % 2, r % 2
    zh, x = c // 4, c % 4
    rid = lambda y, zl, k: lax.rem(y + 8, 4) * 4 + zl * 2 + k
    cid = lambda zh, x: lax.rem(zh + 8, 4) * 4 + lax.rem(x + 8, 4)
    y_right, y_left = (rid(y + 1, zl, k), c), (rid(y - 1, zl, k), c)
    pair, sibling = (rid(y, 1 - zl, k), c), (rid(y, zl, 1 - k), c)
    wrap = lambda v: lax.rem(v + 8, 4)
    x_right, x_left = (r, cid(zh, x + 1)), (r, cid(zh, x - 1))
    z_right, z_left = (r, cid(zh + 1, x)), (r, cid(zh - 1, x))

    mine = 2 * zl + k
    pick = lambda odd, a, b: jnp.where(lax.rem(odd, 2) == 1, a, b)
    shift = lambda q, v: pick(v, jnp.where(q < 2, 3 - q, q - 2), jnp.where(q == 0, 0, jnp.where(q == 1, 3, q - 1)))
    unshift = lambda d, v: pick(v, jnp.where(d < 2, d + 2, 3 - d), jnp.where(d == 0, 0, jnp.where(d == 3, 1, d + 1)))
    t1_to = (rid(y, x // 2, lax.rem(x, 2)), cid(zh + shift(mine, x), x + zh + y))
    far = wrap(x - mine - y)
    off = unshift(wrap(zh - far), mine)
    t1_from = (rid(y, off // 2, lax.rem(off, 2)), far * 4 + mine)
    t1_stays = (t1_to[0] == r) & (t1_to[1] == c)
    t2_to = (rid(far, zl, k), c)
    t2_stays = far == y

    barrier = pltpu.get_barrier_semaphore()

    def greet(i, _):
        pl.semaphore_signal(barrier, inc=1, device_id=(lax.rem(r + i, 16), c), device_id_type=MESH)
        pl.semaphore_signal(barrier, inc=1, device_id=(r, lax.rem(c + i, 16)), device_id_type=MESH)
        return 0

    lax.fori_loop(1, 16, greet, 0)

    @pl.when(jnp.logical_not(t1_stays))
    def _():
        pl.semaphore_signal(barrier, inc=1, device_id=t1_to, device_id_type=MESH)
        pl.semaphore_signal(barrier, inc=1, device_id=t1_from, device_id_type=MESH)

    loads = []
    for d in range(4):
        for zo in range(4):
            owner = zo * 4 + lax.rem(x + d, 4)
            loads.append(
                pltpu.make_async_copy(
                    inv_in.at[pl.ds(pl.multiple_of(owner * 64, 64), 64)],
                    inv.at[d, pl.ds(zo * 64, 64)],
                    loc.at[d],
                )
            )
    for load in loads:
        load.start()
    fold_load = pltpu.make_async_copy(fold_in, fold, loc.at[4])
    fold_load.start()

    for j in range(8):
        g_t[j * 128 : (j + 1) * 128, :] = g_ref[:, j * 128 : (j + 1) * 128].T
    row[...] = jnp.zeros_like(row)
    row[:, 0:64] = jnp.broadcast_to(cw_ref[...].astype(f32), (8, 64))
    tab1[r] = row[...]

    pl.semaphore_wait(barrier, jnp.where(t1_stays, 30, 32))

    sent = []

    def send(src, dst, ssem, rsem, device):
        copy = pltpu.make_async_remote_copy(
            src_ref=src, dst_ref=dst, send_sem=ssem, recv_sem=rsem, device_id=device, device_id_type=MESH
        )
        copy.start()
        sent.append(copy)

    def landed(dst, rsem):
        pltpu.make_async_copy(dst, dst, rsem).wait()

    quarter = lambda ref, h: ref.at[pl.ds(h * 256, 256)]
    p_half = lambda slot, h: pall.at[slot, pl.ds(h * 512, 512)]

    def step(h, src, dst, ssem, rsem, device):
        return pltpu.make_async_remote_copy(
            src_ref=src, dst_ref=dst, send_sem=ssem, recv_sem=rsem, device_id=device, device_id_type=MESH
        )

    t1 = lambda h: step(h, quarter(g_t, h), quarter(t_mid, h), t_send.at[0], t_recv.at[h], t1_to)
    t2 = lambda h: step(h, quarter(t_mid, h), quarter(pall.at[c], h), t_send.at[1], p_recv.at[c, h // 2], t2_to)

    @pl.when(jnp.logical_not(t1_stays))
    def _():
        for h in range(4):
            t1(h).start()

    @pl.when(t1_stays)
    def _():
        for h in range(4):
            pltpu.make_async_copy(quarter(g_t, h), quarter(t_mid, h), t_recv.at[h]).start()

    def t_pass():
        for h in range(4):
            landed(quarter(t_mid, h), t_recv.at[h])

            @pl.when(jnp.logical_not(t2_stays))
            def _():
                t2(h).start()

            @pl.when(t2_stays)
            def _():
                pltpu.make_async_copy(quarter(t_mid, h), quarter(pall.at[c], h), p_recv.at[c, h // 2]).start()

    class Crow:
        def __init__(self, own, buf, depth, cut, ssem, rsem):
            self.own, self.buf, self.depth, self.cut = own, buf, depth, cut
            self.ssem, self.rsem = ssem, rsem

        def rows(self, h):
            return (0, self.cut) if h == 0 else (self.cut, self.depth - self.cut)

        def at(self, slot, h):
            start, size = self.rows(h)
            return self.buf.at[pl.ds(pl.multiple_of(slot * self.depth + start, 16), size)]

        def push(self, slot, h, device, own=False):
            start, size = self.rows(h)
            src = self.own.at[pl.ds(start, size)] if own else self.at(slot, h)
            send(src, self.at(slot, h), self.ssem, self.rsem.at[slot, h], device)

        def got(self, slot, h):
            landed(self.at(slot, h), self.rsem.at[slot, h])

        def start_pair(self):
            for h in (0, 1):
                self.push(r, h, pair, own=True)

        def start_ring(self):
            for h in (0, 1):
                self.push(r, h, y_right, own=True)
                self.push(r, 1 - h, y_left, own=True)

        def start_sibling(self):
            for h in (0, 1):
                self.push(r, h, sibling, own=True)

        def pass_pair(self):
            slot = rid(y, 1 - zl, k)
            for h in (0, 1):
                self.got(slot, h)
            for h in (0, 1):
                self.push(slot, h, y_right)
                self.push(slot, 1 - h, y_left)
            for h in (0, 1):
                self.push(slot, h, sibling)

        def pass_ring(self, zl):
            a, b = rid(y - 1, zl, k), rid(y + 1, zl, k)
            self.got(a, 0)
            self.push(a, 0, y_right)
            self.got(b, 1)
            self.push(b, 1, y_left)
            self.push(a, 0, sibling)
            self.push(b, 1, sibling)
            self.got(a, 1)
            self.push(a, 1, sibling)
            self.got(b, 0)
            self.push(b, 0, sibling)

        def end_ring(self, zl):
            a = rid(y + 2, zl, k)
            for h in (0, 1):
                self.got(a, h)
                self.push(a, h, sibling)

        def end(self):
            for dy in range(4):
                for z in (0, 1):
                    for h in (0, 1):
                        self.got(rid(y + dy, z, 1 - k), h)
            start = pl.multiple_of(r * self.depth, 16)
            self.buf[pl.ds(start, self.depth), :] = self.own[...]

    heads = Crow(head_t, hall, 80, 48, h_send, h_recv)
    grads = Crow(g_ref, call, 128, 64, g_send, g_recv)

    def weights_out(i, _):
        pltpu.make_async_remote_copy(
            src_ref=row, dst_ref=tab1.at[r], send_sem=w_send, recv_sem=w1_recv.at[r],
            device_id=(lax.rem(r + i, 16), c), device_id_type=MESH,
        ).start()
        return 0

    def p_push(slot, h, device):
        send(p_half(slot, h), p_half(slot, h), p_send, p_recv.at[slot, h], device)

    def p_got(slot, h):
        landed(p_half(slot, h), p_recv.at[slot, h])

    def p_start():
        p_got(c, 0)
        p_push(c, 0, z_right)
        p_push(c, 0, x_right)
        p_got(c, 1)
        p_push(c, 1, z_left)
        p_push(c, 1, x_left)
        p_push(c, 1, z_right)
        p_push(c, 0, z_left)
        p_push(c, 1, x_right)
        p_push(c, 0, x_left)

    def z_pass():
        a, b = cid(zh - 1, x), cid(zh + 1, x)
        p_got(a, 0)
        p_push(a, 0, z_right)
        p_got(b, 1)
        p_push(b, 1, z_left)
        p_got(a, 1)
        for h in (0, 1):
            p_push(a, h, x_right)
            p_push(a, 1 - h, x_left)
        p_got(b, 0)
        for h in (0, 1):
            p_push(b, h, x_right)
            p_push(b, 1 - h, x_left)

    def x_pass(dz):
        a, b = cid(zh + dz, x - 1), cid(zh + dz, x + 1)
        p_got(a, 0)
        p_push(a, 0, x_right)
        p_got(b, 1)
        p_push(b, 1, x_left)

    def x_end(dz):
        a, b, o = cid(zh + dz, x - 1), cid(zh + dz, x + 1), cid(zh + dz, x + 2)
        p_got(a, 1)
        p_got(b, 0)
        p_got(o, 0)
        p_got(o, 1)

    def z_end():
        a = cid(zh + 2, x)
        for h in (0, 1):
            p_got(a, h)
            p_push(a, h, x_right)
            p_push(a, h, x_left)

    def dot_heads(left, cols):
        return lax.dot_general(left, hall[cols, :], (((1,), (1,)), ((), ())), preferred_element_type=f32)

    def products_x(d):
        def tile(j, _):
            cols = pl.ds(pl.multiple_of(j * 256, 256), 256)
            part_x[d, :, cols] = dot_heads(inv[d], cols)
            return 0

        lax.fori_loop(0, split // 256, tile, 0)

    def products_z(d):
        rows = pl.ds(pl.multiple_of(lax.rem(zh + d, 4) * 64, 64), 64)
        left = jnp.concatenate([inv[dx, rows, :] for dx in range(4)], axis=0)

        def tile(j, _):
            cols = pl.ds(pl.multiple_of(j * 256, 256), 256)
            part_z[d, :, cols] = dot_heads(left, pl.ds(pl.multiple_of(split + j * 256, 256), 256))
            return 0

        lax.fori_loop(0, (1280 - split) // 256, tile, 0)

    class Reduce:
        def __init__(self, term, left, right, qs, qr, ss, sr, ssem, qsem, usem):
            self.term, self.to = term, (left, right)
            self.qs, self.qr, self.ss, self.sr = qs, qr, ss, sr
            self.ssem, self.qsem, self.usem = ssem, qsem, usem

        def push(self, way, m, value):
            most = jnp.maximum(jnp.max(jnp.abs(value)), 1e-30)
            self.qs[way, m] = jnp.round(value * (top / most)).astype(i32).astype(i16)
            self.ss[way, m] = jnp.full((8, 128), most / top, f32)
            for src, dst, sem in ((self.qs, self.qr, self.qsem), (self.ss, self.sr, self.usem)):
                send(src.at[way, m], dst.at[way, m], self.ssem, sem.at[way, m], self.to[way])

        def pull(self, way, m):
            landed(self.qr.at[way, m], self.qsem.at[way, m])
            landed(self.sr.at[way, m], self.usem.at[way, m])
            unit = self.sr[way, m][0:1, 0:1]
            return self.qr[way, m].astype(i32).astype(f32) * unit

        def first(self):
            self.push(0, 0, self.term(2, 0))
            self.push(1, 0, self.term(2, 1))

        def second(self):
            self.push(0, 1, self.term(3, 1))
            self.push(1, 1, self.term(1, 0))

        def third(self):
            self.push(0, 2, self.term(3, 0) + self.pull(0, 0))
            self.push(1, 2, self.term(1, 1) + self.pull(1, 0))

        def last(self, p):
            own = self.term(0, p)
            return own + self.pull(0, 2 if p == 0 else 1) + self.pull(1, 1 if p == 0 else 2)

        def total(self, ref):
            for p in (0, 1):
                ref[p * 128 : (p + 1) * 128, :] = self.last(p)

        def result(self, cols):
            for p in (0, 1):
                pre_ref[p * 32 : (p + 1) * 32, cols] = self.last(p).astype(bf16)

    def z_term(d, p):
        start = lax.rem(zh + d, 4) * 64 + p * 32
        return total_z[pl.ds(pl.multiple_of(start, 32), 32), :]

    x_first = Reduce(lambda d, p: part_x[d, p * 128 : (p + 1) * 128, :], x_left, x_right, *moves[0])
    then_z = Reduce(z_term, z_left, z_right, *moves[1])
    z_first = Reduce(lambda d, p: part_z[d, p * 128 : (p + 1) * 128, :], z_left, z_right, *moves[2])
    then_x = Reduce(lambda d, p: total_x[d * 64 + p * 32 : d * 64 + p * 32 + 32, :], x_left, x_right, *moves[3])

    def weights_in(i, _):
        slot = lax.rem(r + i, 16)
        landed(tab1.at[slot], w1_recv.at[slot])
        return 0

    def weights_on(i, _):
        pltpu.make_async_remote_copy(
            src_ref=tabc, dst_ref=tab2.at[c], send_sem=w_send, recv_sem=w2_recv.at[c],
            device_id=(r, lax.rem(c + i, 16)), device_id_type=MESH,
        ).start()
        return 0

    def weights_all(i, _):
        slot = lax.rem(c + i, 16)
        landed(tab2.at[slot], w2_recv.at[slot])
        return 0

    heads.start_pair()
    heads.start_ring()
    lax.fori_loop(1, 16, weights_out, 0)
    t_pass()
    heads.pass_ring(zl)
    heads.pass_pair()
    heads.start_sibling()
    grads.start_pair()
    p_start()
    heads.pass_ring(1 - zl)
    grads.start_ring()
    heads.end_ring(zl)
    heads.end_ring(1 - zl)
    grads.pass_pair()
    grads.start_sibling()
    heads.end()
    for load in loads:
        load.wait()
    products_x(2)
    x_first.first()
    products_x(3)
    products_x(1)
    x_pass(0)
    products_z(2)
    x_first.second()
    z_first.first()
    lax.fori_loop(1, 16, weights_in, 0)
    tabc[...] = tab1[:, 0, :]
    tab2[c] = tabc[...]
    lax.fori_loop(1, 16, weights_on, 0)
    grads.pass_ring(1 - zl)
    grads.pass_ring(zl)
    x_first.third()
    products_z(3)
    z_pass()
    x_end(0)
    products_x(0)
    grads.end_ring(1 - zl)
    products_z(1)
    z_first.second()
    products_z(0)
    grads.end_ring(zl)
    z_first.third()
    x_first.total(total_z)
    grads.end()
    lax.fori_loop(1, 16, weights_all, 0)

    table = tab2[...].reshape(256, 128).astype(i32)
    table_hi = ((table >> 5) << 5).astype(f32).astype(bf16)
    table_lo = (table & 31).astype(f32).astype(bf16)
    lanes = lax.broadcasted_iota(i32, (128, 256), 1)
    lane = lax.broadcasted_iota(i32, (128, 128), 1)

    def weigh(b, weight_sum):
        held = wrap(lax.rem(b, 4) - mine - y) * 4 + unshift(wrap(b // 4 - y), mine)
        lab = jnp.broadcast_to(lab_ref[pl.ds(held, 1), :].astype(f32), (128, 128)).T.astype(i32)
        at = ((lab >> 6) & 15) * 16 + (lab >> 10)
        hot = (lanes == jnp.concatenate([at, at], axis=1)).astype(f32).astype(bf16)
        picked = jnp.dot(hot, table_hi, preferred_element_type=f32)
        picked += jnp.dot(hot, table_lo, preferred_element_type=f32)
        weight = jnp.sum(jnp.where(lane == (lab & 63), picked, 0.0), axis=1, keepdims=True) / weight_unit
        rows = pl.ds(pl.multiple_of(held * 128, 128), 128)
        wt[pl.ds(pl.multiple_of(b * 128, 128), 128), :] = (weight * call[rows, :].astype(f32)).astype(bf16)
        return weight_sum + jnp.sum(weight)

    weight_sum = lax.fori_loop(0, 6, weigh, jnp.float32(0.0))
    then_z.second()
    z_end()
    then_z.first()
    x_pass(-1)
    weight_sum = lax.fori_loop(6, 11, weigh, weight_sum)
    weight_sum = lax.fori_loop(11, 16, weigh, weight_sum)
    gram_unit = (1.0 - stat_decay) / weight_sum
    fold_load.wait()

    def gram(sets, i, j):
        value = None
        for dz in sets:
            first = lax.rem(zh + dz + 8, 4) * 4
            left = jnp.concatenate([pall[first + q, pl.ds(i * 512, 512), :] for q in range(4)], axis=1)
            right = wt[pl.ds(pl.multiple_of(first * 128, 512), 512), pl.ds(pl.multiple_of(j * 256, 256), 256)]
            term = jnp.dot(left, right, preferred_element_type=f32)
            value = term if value is None else value + term
        return value

    def gram_early(sets):
        def tile(j, _):
            cols = pl.ds(pl.multiple_of(j * 256, 256), 256)
            for i in range(2):
                rows = pl.ds(i * 512, 512)
                old = fold[rows, cols]
                if sets[0] == 0:
                    old = stat_decay * old
                fold[rows, cols] = old + gram_unit * gram(sets, i, j)
            return 0

        lax.fori_loop(0, 4, tile, 0)

    gram_early((0,))
    z_first.total(total_x)
    x_pass(1)
    then_x.first()
    then_x.second()
    x_pass(2)
    then_z.third()
    x_end(-1)
    gram_early((-1,))
    then_x.third()
    x_end(1)
    gram_early((1,))
    then_z.result(slice(0, split))
    x_end(2)
    then_x.result(slice(split, 1280))
    stores = []
    for i in range(2):
        rows = pl.ds(i * 512, 512)

        def gram_late(j, _):
            cols = pl.ds(pl.multiple_of(j * 256, 256), 256)
            fold[rows, cols] += gram_unit * gram((2,), i, j)
            return 0

        lax.fori_loop(0, 4, gram_late, 0)
        store = pltpu.make_async_copy(fold.at[rows], fout.at[rows], loc.at[5 + i])
        store.start()
        stores.append(store)

    for copy in sent:
        copy.wait_send()

    @pl.when(jnp.logical_not(t1_stays))
    def _():
        for h in range(4):
            t1(h).wait_send()

    @pl.when(jnp.logical_not(t2_stays))
    def _():
        for h in range(4):
            t2(h).wait_send()

    def weights_left(i, _):
        pltpu.make_async_remote_copy(
            src_ref=row, dst_ref=tab1.at[r], send_sem=w_send, recv_sem=w1_recv.at[r],
            device_id=(lax.rem(r + i, 16), c), device_id_type=MESH,
        ).wait_send()
        pltpu.make_async_remote_copy(
            src_ref=tabc, dst_ref=tab2.at[c], send_sem=w_send, recv_sem=w2_recv.at[c],
            device_id=(r, lax.rem(c + i, 16)), device_id_type=MESH,
        ).wait_send()
        return 0

    lax.fori_loop(1, 16, weights_left, 0)
    for store in stores:
        store.wait()


def messages(rows, columns):
    dma = pltpu.SemaphoreType.DMA
    return (
        *[pltpu.VMEM((2, 3, rows, columns), i16)] * 2,
        *[pltpu.VMEM((2, 3, 8, 128), f32)] * 2,
        dma,
        dma((2, 3)),
        dma((2, 3)),
    )


def body(grad_rows, labels, class_weights, factor_old, inverse_old, head_grad):
    vmem, anywhere = pl.BlockSpec(memory_space=pltpu.VMEM), pl.BlockSpec(memory_space=pl.ANY)
    dma = pltpu.SemaphoreType.DMA
    factor_new, preconditioned = pl.pallas_call(
        kernel,
        out_shape=(
            jax.ShapeDtypeStruct((1024, 1024), f32),
            jax.ShapeDtypeStruct((64, 1280), bf16),
        ),
        in_specs=[vmem, vmem, vmem, vmem, anywhere, anywhere],
        out_specs=(anywhere, vmem),
        scratch_shapes=[
            pltpu.VMEM((1024, 128), bf16),
            pltpu.VMEM((1024, 128), bf16),
            pltpu.VMEM((1280, 1024), bf16),
            pltpu.VMEM((2048, 1024), bf16),
            pltpu.VMEM((16, 1024, 128), bf16),
            pltpu.VMEM((2048, 1024), bf16),
            pltpu.VMEM((4, 256, 1024), bf16),
            pltpu.VMEM((1024, 1024), f32),
            pltpu.VMEM((4, 256, split), f32),
            pltpu.VMEM((256, split), f32),
            pltpu.VMEM((4, 256, 1280 - split), f32),
            pltpu.VMEM((256, 1280 - split), f32),
            *messages(128, split),
            *messages(32, split),
            *messages(128, 1280 - split),
            *messages(32, 1280 - split),
            pltpu.VMEM((8, 128), f32),
            pltpu.VMEM((16, 8, 128), f32),
            pltpu.VMEM((16, 128), f32),
            pltpu.VMEM((16, 16, 128), f32),
                dma, dma((16, 2)), dma, dma((16, 2)), dma, dma((16, 2)),
            dma((2,)), dma((4,)), dma, dma((16,)), dma((16,)),
            dma((7,)),
        ],
        compiler_params=pltpu.CompilerParams(
            collective_id=0, has_side_effects=True, vmem_limit_bytes=58 << 20
        ),
        name="kfac",
    )(
        grad_rows,
        head_grad.T,
        labels.reshape(16, 128),
        class_weights.reshape(1, 64),
        factor_old,
        inverse_old,
    )
    return factor_new, preconditioned


def solution(mesh):
    placed = (
        P("crow", "ccol"),
        P(),
        P(("crow", "ccol")),
        P("crow", "ccol"),
        P("crow", "ccol"),
        P("ccol", "crow"),
    )
    return jax.shard_map(
        body,
        mesh=mesh,
        in_specs=placed,
        out_specs=(P("crow", "ccol"), P(("crow", "ccol"), None)),
        check_vma=False,
    )
```

```python
import jax
import jax.numpy as jnp
from jax import lax
from jax.experimental import pallas as pl
from jax.experimental.pallas import tpu as pltpu
from jax.sharding import PartitionSpec as P

stat_decay = 0.75
weight_unit = 1024.0
MESH = pl.DeviceIdType.MESH
f32, bf16, i32, i16 = jnp.float32, jnp.bfloat16, jnp.int32, jnp.int16
top = 32767.0
split = 768


def kernel(
    g_ref, head_t, lab_ref, cw_ref, fold_in, inv_in,
    fout, pre_ref,
    g_t, t_mid, hall, call, pall, wt, inv, fold, part_x, total_z, part_z, total_x,
    *rest,
):
    moves, rest = [rest[i * 7 : i * 7 + 7] for i in range(4)], rest[28:]
    row, tab1, tabc, tab2, h_send, h_recv, g_send, g_recv, p_send, p_recv, *rest = rest
    t_send, t_recv, w_send, w1_recv, w2_recv, loc = rest
    r, c = lax.axis_index("crow"), lax.axis_index("ccol")
    y, zl, k = r // 4, (r // 2) % 2, r % 2
    zh, x = c // 4, c % 4
    rid = lambda y, zl, k: lax.rem(y + 8, 4) * 4 + zl * 2 + k
    cid = lambda zh, x: lax.rem(zh + 8, 4) * 4 + lax.rem(x + 8, 4)
    y_right, y_left = (rid(y + 1, zl, k), c), (rid(y - 1, zl, k), c)
    pair, sibling = (rid(y, 1 - zl, k), c), (rid(y, zl, 1 - k), c)
    wrap = lambda v: lax.rem(v + 8, 4)
    x_right, x_left = (r, cid(zh, x + 1)), (r, cid(zh, x - 1))
    z_right, z_left = (r, cid(zh + 1, x)), (r, cid(zh - 1, x))

    mine = 2 * zl + k
    pick = lambda odd, a, b: jnp.where(lax.rem(odd, 2) == 1, a, b)
    shift = lambda q, v: pick(v, jnp.where(q < 2, 3 - q, q - 2), jnp.where(q == 0, 0, jnp.where(q == 1, 3, q - 1)))
    unshift = lambda d, v: pick(v, jnp.where(d < 2, d + 2, 3 - d), jnp.where(d == 0, 0, jnp.where(d == 3, 1, d + 1)))
    t1_to = (rid(y, x // 2, lax.rem(x, 2)), cid(zh + shift(mine, x), x + zh + y))
    far = wrap(x - mine - y)
    off = unshift(wrap(zh - far), mine)
    t1_from = (rid(y, off // 2, lax.rem(off, 2)), far * 4 + mine)
    t1_stays = (t1_to[0] == r) & (t1_to[1] == c)
    t2_to = (rid(far, zl, k), c)
    t2_stays = far == y

    barrier = pltpu.get_barrier_semaphore()

    def greet(i, _):
        pl.semaphore_signal(barrier, inc=1, device_id=(lax.rem(r + i, 16), c), device_id_type=MESH)
        pl.semaphore_signal(barrier, inc=1, device_id=(r, lax.rem(c + i, 16)), device_id_type=MESH)
        return 0

    lax.fori_loop(1, 16, greet, 0)

    @pl.when(jnp.logical_not(t1_stays))
    def _():
        pl.semaphore_signal(barrier, inc=1, device_id=t1_to, device_id_type=MESH)
        pl.semaphore_signal(barrier, inc=1, device_id=t1_from, device_id_type=MESH)

    for j in range(8):
        g_t[j * 128 : (j + 1) * 128, :] = g_ref[:, j * 128 : (j + 1) * 128].T
    units = jnp.broadcast_to(cw_ref[...], (8, 64))
    row[:, 0:64] = ((units >> 5) << 5).astype(f32)
    row[:, 64:128] = (units & 31).astype(f32)
    tab1[r] = row[...]

    pl.semaphore_wait(barrier, jnp.where(t1_stays, 30, 32))

    sent = []

    def send(src, dst, ssem, rsem, device):
        copy = pltpu.make_async_remote_copy(
            src_ref=src, dst_ref=dst, send_sem=ssem, recv_sem=rsem, device_id=device, device_id_type=MESH
        )
        copy.start()
        sent.append(copy)

    def landed(dst, rsem):
        pltpu.make_async_copy(dst, dst, rsem).wait()

    quarter = lambda ref, h: ref.at[pl.ds(h * 256, 256)]
    p_half = lambda slot, h: pall.at[slot, pl.ds(h * 512, 512)]

    def step(h, src, dst, ssem, rsem, device):
        return pltpu.make_async_remote_copy(
            src_ref=src, dst_ref=dst, send_sem=ssem, recv_sem=rsem, device_id=device, device_id_type=MESH
        )

    t1 = lambda h: step(h, quarter(g_t, h), quarter(t_mid, h), t_send.at[0], t_recv.at[h], t1_to)
    t2 = lambda h: step(h, quarter(t_mid, h), quarter(pall.at[c], h), t_send.at[1], p_recv.at[c, h // 2], t2_to)

    @pl.when(jnp.logical_not(t1_stays))
    def _():
        for h in range(4):
            t1(h).start()

    @pl.when(t1_stays)
    def _():
        for h in range(4):
            pltpu.make_async_copy(quarter(g_t, h), quarter(t_mid, h), t_recv.at[h]).start()

    def t_pass():
        for h in range(4):
            landed(quarter(t_mid, h), t_recv.at[h])

            @pl.when(jnp.logical_not(t2_stays))
            def _():
                t2(h).start()

            @pl.when(t2_stays)
            def _():
                pltpu.make_async_copy(quarter(t_mid, h), quarter(pall.at[c], h), p_recv.at[c, h // 2]).start()

    class Crow:
        def __init__(self, own, buf, depth, cut, ssem, rsem):
            self.own, self.buf, self.depth, self.cut = own, buf, depth, cut
            self.ssem, self.rsem = ssem, rsem

        def rows(self, h):
            return (0, self.cut) if h == 0 else (self.cut, self.depth - self.cut)

        def at(self, slot, h):
            start, size = self.rows(h)
            return self.buf.at[pl.ds(pl.multiple_of(slot * self.depth + start, 16), size)]

        def push(self, slot, h, device, own=False):
            start, size = self.rows(h)
            src = self.own.at[pl.ds(start, size)] if own else self.at(slot, h)
            send(src, self.at(slot, h), self.ssem, self.rsem.at[slot, h], device)

        def got(self, slot, h):
            landed(self.at(slot, h), self.rsem.at[slot, h])

        def start_pair(self):
            for h in (0, 1):
                self.push(r, h, pair, own=True)

        def start_ring(self):
            for h in (0, 1):
                self.push(r, h, y_right, own=True)
                self.push(r, 1 - h, y_left, own=True)

        def start_sibling(self):
            for h in (0, 1):
                self.push(r, h, sibling, own=True)

        def pass_pair(self):
            slot = rid(y, 1 - zl, k)
            for h in (0, 1):
                self.got(slot, h)
            for h in (0, 1):
                self.push(slot, h, y_right)
                self.push(slot, 1 - h, y_left)
            for h in (0, 1):
                self.push(slot, h, sibling)

        def pass_ring(self, zl):
            a, b = rid(y - 1, zl, k), rid(y + 1, zl, k)
            self.got(a, 0)
            self.push(a, 0, y_right)
            self.got(b, 1)
            self.push(b, 1, y_left)
            self.push(a, 0, sibling)
            self.push(b, 1, sibling)
            self.got(a, 1)
            self.push(a, 1, sibling)
            self.got(b, 0)
            self.push(b, 0, sibling)

        def end_ring(self, zl):
            a = rid(y + 2, zl, k)
            for h in (0, 1):
                self.got(a, h)
                self.push(a, h, sibling)

        def end(self):
            for dy in range(4):
                for z in (0, 1):
                    for h in (0, 1):
                        self.got(rid(y + dy, z, 1 - k), h)
            start = pl.multiple_of(r * self.depth, 16)
            self.buf[pl.ds(start, self.depth), :] = self.own[...]

    heads = Crow(head_t, hall, 80, 48, h_send, h_recv)
    grads = Crow(g_ref, call, 128, 64, g_send, g_recv)

    loads = []
    for d in range(4):
        for zo in range(4):
            owner = zo * 4 + lax.rem(x + d, 4)
            loads.append(
                pltpu.make_async_copy(
                    inv_in.at[pl.ds(pl.multiple_of(owner * 64, 64), 64)],
                    inv.at[d, pl.ds(zo * 64, 64)],
                    loc.at[d],
                )
            )
    fold_load = pltpu.make_async_copy(fold_in, fold, loc.at[4])

    def weights_out(i, _):
        pltpu.make_async_remote_copy(
            src_ref=row, dst_ref=tab1.at[r], send_sem=w_send, recv_sem=w1_recv.at[r],
            device_id=(lax.rem(r + i, 16), c), device_id_type=MESH,
        ).start()
        return 0

    def p_push(slot, h, device):
        send(p_half(slot, h), p_half(slot, h), p_send, p_recv.at[slot, h], device)

    def p_got(slot, h):
        landed(p_half(slot, h), p_recv.at[slot, h])

    def p_start():
        p_got(c, 0)
        p_push(c, 0, z_right)
        p_push(c, 0, x_right)
        p_got(c, 1)
        p_push(c, 1, z_left)
        p_push(c, 1, x_left)
        p_push(c, 1, z_right)
        p_push(c, 0, z_left)
        p_push(c, 1, x_right)
        p_push(c, 0, x_left)

    def z_pass():
        a, b = cid(zh - 1, x), cid(zh + 1, x)
        p_got(a, 0)
        p_push(a, 0, z_right)
        p_got(b, 1)
        p_push(b, 1, z_left)
        p_got(a, 1)
        for h in (0, 1):
            p_push(a, h, x_right)
            p_push(a, 1 - h, x_left)
        p_got(b, 0)
        for h in (0, 1):
            p_push(b, h, x_right)
            p_push(b, 1 - h, x_left)

    def x_pass(dz):
        a, b = cid(zh + dz, x - 1), cid(zh + dz, x + 1)
        p_got(a, 0)
        p_push(a, 0, x_right)
        p_got(b, 1)
        p_push(b, 1, x_left)

    def x_end(dz):
        a, b, o = cid(zh + dz, x - 1), cid(zh + dz, x + 1), cid(zh + dz, x + 2)
        p_got(a, 1)
        p_got(b, 0)
        p_got(o, 0)
        p_got(o, 1)

    def z_end():
        a = cid(zh + 2, x)
        for h in (0, 1):
            p_got(a, h)
            p_push(a, h, x_right)
            p_push(a, h, x_left)

    def dot_heads(left, cols):
        return lax.dot_general(left, hall[cols, :], (((1,), (1,)), ((), ())), preferred_element_type=f32)

    def products_x(d):
        def tile(j, _):
            cols = pl.ds(pl.multiple_of(j * 256, 256), 256)
            part_x[d, :, cols] = dot_heads(inv[d], cols)
            return 0

        lax.fori_loop(0, split // 256, tile, 0)

    def products_z(d):
        rows = pl.ds(pl.multiple_of(lax.rem(zh + d, 4) * 64, 64), 64)
        left = jnp.concatenate([inv[dx, rows, :] for dx in range(4)], axis=0)

        def tile(j, _):
            cols = pl.ds(pl.multiple_of(j * 256, 256), 256)
            part_z[d, :, cols] = dot_heads(left, pl.ds(pl.multiple_of(split + j * 256, 256), 256))
            return 0

        lax.fori_loop(0, (1280 - split) // 256, tile, 0)

    class Reduce:
        def __init__(self, term, left, right, qs, qr, ss, sr, ssem, qsem, usem):
            self.term, self.to = term, (left, right)
            self.qs, self.qr, self.ss, self.sr = qs, qr, ss, sr
            self.ssem, self.qsem, self.usem = ssem, qsem, usem

        def push(self, way, m, value):
            most = jnp.maximum(jnp.max(jnp.abs(value)), 1e-30)
            self.qs[way, m] = jnp.round(value * (top / most)).astype(i32).astype(i16)
            self.ss[way, m] = jnp.full((8, 128), most / top, f32)
            for src, dst, sem in ((self.qs, self.qr, self.qsem), (self.ss, self.sr, self.usem)):
                send(src.at[way, m], dst.at[way, m], self.ssem, sem.at[way, m], self.to[way])

        def pull(self, way, m):
            landed(self.qr.at[way, m], self.qsem.at[way, m])
            landed(self.sr.at[way, m], self.usem.at[way, m])
            unit = self.sr[way, m][0:1, 0:1]
            return self.qr[way, m].astype(i32).astype(f32) * unit

        def first(self):
            self.push(0, 0, self.term(2, 0))
            self.push(1, 0, self.term(2, 1))

        def second(self):
            self.push(0, 1, self.term(3, 1))
            self.push(1, 1, self.term(1, 0))

        def third(self):
            self.push(0, 2, self.term(3, 0) + self.pull(0, 0))
            self.push(1, 2, self.term(1, 1) + self.pull(1, 0))

        def last(self, p):
            own = self.term(0, p)
            return own + self.pull(0, 2 if p == 0 else 1) + self.pull(1, 1 if p == 0 else 2)

        def total(self, ref):
            for p in (0, 1):
                ref[p * 128 : (p + 1) * 128, :] = self.last(p)

        def result(self, cols):
            for p in (0, 1):
                pre_ref[p * 32 : (p + 1) * 32, cols] = self.last(p).astype(bf16)

    def z_term(d, p):
        start = lax.rem(zh + d, 4) * 64 + p * 32
        return total_z[pl.ds(pl.multiple_of(start, 32), 32), :]

    x_first = Reduce(lambda d, p: part_x[d, p * 128 : (p + 1) * 128, :], x_left, x_right, *moves[0])
    then_z = Reduce(z_term, z_left, z_right, *moves[1])
    z_first = Reduce(lambda d, p: part_z[d, p * 128 : (p + 1) * 128, :], z_left, z_right, *moves[2])
    then_x = Reduce(lambda d, p: total_x[d * 64 + p * 32 : d * 64 + p * 32 + 32, :], x_left, x_right, *moves[3])

    def weights_in(i, _):
        slot = lax.rem(r + i, 16)
        landed(tab1.at[slot], w1_recv.at[slot])
        return 0

    def weights_on(i, _):
        pltpu.make_async_remote_copy(
            src_ref=tabc, dst_ref=tab2.at[c], send_sem=w_send, recv_sem=w2_recv.at[c],
            device_id=(r, lax.rem(c + i, 16)), device_id_type=MESH,
        ).start()
        return 0

    def weights_all(i, _):
        slot = lax.rem(c + i, 16)
        landed(tab2.at[slot], w2_recv.at[slot])
        return 0

    heads.start_pair()
    heads.start_ring()
    for load in loads:
        load.start()
    fold_load.start()
    lax.fori_loop(1, 16, weights_out, 0)
    t_pass()
    heads.pass_ring(zl)
    heads.pass_pair()
    heads.start_sibling()
    grads.start_pair()
    p_start()
    heads.pass_ring(1 - zl)
    grads.start_ring()
    heads.end_ring(zl)
    lax.fori_loop(1, 16, weights_in, 0)
    tabc[...] = tab1[:, 0, :].astype(bf16)
    tab2[c] = tabc[...]
    lax.fori_loop(1, 16, weights_on, 0)
    heads.end_ring(1 - zl)
    grads.pass_pair()
    grads.start_sibling()
    heads.end()
    for load in loads:
        load.wait()
    products_x(2)
    x_first.first()
    products_x(3)
    products_x(1)
    x_pass(0)
    products_z(2)
    x_first.second()
    z_first.first()
    grads.pass_ring(zl)
    grads.pass_ring(1 - zl)
    z_pass()
    x_end(0)
    products_z(3)
    x_first.third()
    products_x(0)
    grads.end_ring(1 - zl)
    products_z(1)
    z_first.second()
    products_z(0)
    grads.end_ring(zl)
    x_pass(-1)
    z_first.third()
    z_end()
    grads.end()
    lax.fori_loop(1, 16, weights_all, 0)

    table = tab2[...].reshape(256, 128)
    lanes = lax.broadcasted_iota(i32, (128, 256), 1)
    lane = lax.broadcasted_iota(i32, (128, 128), 1)

    def weigh(b, weight_sum):
        held = wrap(lax.rem(b, 4) - mine - y) * 4 + unshift(wrap(b // 4 - y), mine)
        lab = jnp.broadcast_to(lab_ref[pl.ds(held, 1), :].astype(f32), (128, 128)).T.astype(i32)
        at = ((lab >> 6) & 15) * 16 + (lab >> 10)
        hot = (lanes == jnp.concatenate([at, at], axis=1)).astype(f32).astype(bf16)
        picked = jnp.dot(hot, table, preferred_element_type=f32)
        weight = jnp.sum(jnp.where((lane & 63) == (lab & 63), picked, 0.0), axis=1, keepdims=True) / weight_unit
        rows = pl.ds(pl.multiple_of(held * 128, 128), 128)
        wt[pl.ds(pl.multiple_of(b * 128, 128), 128), :] = (weight * call[rows, :].astype(f32)).astype(bf16)
        return weight_sum + jnp.sum(weight)

    weight_sum = lax.fori_loop(0, 6, weigh, jnp.float32(0.0))
    weight_sum = lax.fori_loop(6, 11, weigh, weight_sum)
    weight_sum = lax.fori_loop(11, 16, weigh, weight_sum)
    gram_unit = (1.0 - stat_decay) / weight_sum
    fold_load.wait()

    def gram(sets, i, j):
        value = None
        for dz in sets:
            first = lax.rem(zh + dz + 8, 4) * 4
            left = jnp.concatenate([pall[first + q, pl.ds(i * 512, 512), :] for q in range(4)], axis=1)
            right = wt[pl.ds(pl.multiple_of(first * 128, 512), 512), pl.ds(pl.multiple_of(j * 256, 256), 256)]
            term = jnp.dot(left, right, preferred_element_type=f32)
            value = term if value is None else value + term
        return value

    def gram_early(sets):
        def tile(j, _):
            cols = pl.ds(pl.multiple_of(j * 256, 256), 256)
            for i in range(2):
                rows = pl.ds(i * 512, 512)
                old = fold[rows, cols]
                if sets[0] == 0:
                    old = stat_decay * old
                fold[rows, cols] = old + gram_unit * gram(sets, i, j)
            return 0

        lax.fori_loop(0, 4, tile, 0)

    x_first.total(total_z)
    then_z.first()
    z_first.total(total_x)
    then_x.first()
    x_pass(1)
    then_x.second()
    then_z.second()
    gram_early((0,))
    then_z.third()
    then_x.third()
    x_pass(2)
    x_end(-1)
    gram_early((-1,))
    x_end(1)
    gram_early((1,))
    then_x.result(slice(split, 1280))
    then_z.result(slice(0, split))
    x_end(2)
    stores = []
    for i in range(2):
        rows = pl.ds(i * 512, 512)

        def gram_late(j, _):
            cols = pl.ds(pl.multiple_of(j * 256, 256), 256)
            fold[rows, cols] += gram_unit * gram((2,), i, j)
            return 0

        lax.fori_loop(0, 4, gram_late, 0)
        store = pltpu.make_async_copy(fold.at[rows], fout.at[rows], loc.at[5 + i])
        store.start()
        stores.append(store)

    for copy in sent:
        copy.wait_send()

    @pl.when(jnp.logical_not(t1_stays))
    def _():
        for h in range(4):
            t1(h).wait_send()

    @pl.when(jnp.logical_not(t2_stays))
    def _():
        for h in range(4):
            t2(h).wait_send()

    def weights_left(i, _):
        pltpu.make_async_remote_copy(
            src_ref=row, dst_ref=tab1.at[r], send_sem=w_send, recv_sem=w1_recv.at[r],
            device_id=(lax.rem(r + i, 16), c), device_id_type=MESH,
        ).wait_send()
        pltpu.make_async_remote_copy(
            src_ref=tabc, dst_ref=tab2.at[c], send_sem=w_send, recv_sem=w2_recv.at[c],
            device_id=(r, lax.rem(c + i, 16)), device_id_type=MESH,
        ).wait_send()
        return 0

    lax.fori_loop(1, 16, weights_left, 0)
    for store in stores:
        store.wait()


def messages(rows, columns):
    dma = pltpu.SemaphoreType.DMA
    return (
        *[pltpu.VMEM((2, 3, rows, columns), i16)] * 2,
        *[pltpu.VMEM((2, 3, 8, 128), f32)] * 2,
        dma,
        dma((2, 3)),
        dma((2, 3)),
    )


def body(grad_rows, labels, class_weights, factor_old, inverse_old, head_grad):
    vmem, anywhere = pl.BlockSpec(memory_space=pltpu.VMEM), pl.BlockSpec(memory_space=pl.ANY)
    dma = pltpu.SemaphoreType.DMA
    factor_new, preconditioned = pl.pallas_call(
        kernel,
        out_shape=(
            jax.ShapeDtypeStruct((1024, 1024), f32),
            jax.ShapeDtypeStruct((64, 1280), bf16),
        ),
        in_specs=[vmem, vmem, vmem, vmem, anywhere, anywhere],
        out_specs=(anywhere, vmem),
        scratch_shapes=[
            pltpu.VMEM((1024, 128), bf16),
            pltpu.VMEM((1024, 128), bf16),
            pltpu.VMEM((1280, 1024), bf16),
            pltpu.VMEM((2048, 1024), bf16),
            pltpu.VMEM((16, 1024, 128), bf16),
            pltpu.VMEM((2048, 1024), bf16),
            pltpu.VMEM((4, 256, 1024), bf16),
            pltpu.VMEM((1024, 1024), f32),
            pltpu.VMEM((4, 256, split), f32),
            pltpu.VMEM((256, split), f32),
            pltpu.VMEM((4, 256, 1280 - split), f32),
            pltpu.VMEM((256, 1280 - split), f32),
            *messages(128, split),
            *messages(32, split),
            *messages(128, 1280 - split),
            *messages(32, 1280 - split),
            pltpu.VMEM((8, 128), f32),
            pltpu.VMEM((16, 8, 128), f32),
            pltpu.VMEM((16, 128), bf16),
            pltpu.VMEM((16, 16, 128), bf16),
                dma, dma((16, 2)), dma, dma((16, 2)), dma, dma((16, 2)),
            dma((2,)), dma((4,)), dma, dma((16,)), dma((16,)),
            dma((7,)),
        ],
        compiler_params=pltpu.CompilerParams(
            collective_id=0, has_side_effects=True, vmem_limit_bytes=58 << 20
        ),
        name="kfac",
    )(
        grad_rows,
        head_grad.T,
        labels.reshape(16, 128),
        class_weights.reshape(1, 64),
        factor_old,
        inverse_old,
    )
    return factor_new, preconditioned


def solution(mesh):
    placed = (
        P("crow", "ccol"),
        P(),
        P(("crow", "ccol")),
        P("crow", "ccol"),
        P("crow", "ccol"),
        P("ccol", "crow"),
    )
    return jax.shard_map(
        body,
        mesh=mesh,
        in_specs=placed,
        out_specs=(P("crow", "ccol"), P(("crow", "ccol"), None)),
        check_vma=False,
    )
```

```python
import jax
import jax.numpy as jnp
from jax import lax
from jax.experimental import pallas as pl
from jax.experimental.pallas import tpu as pltpu
from jax.sharding import PartitionSpec as P

stat_decay = 0.75
weight_unit = 1024.0
MESH = pl.DeviceIdType.MESH
f32, bf16, i32, i16 = jnp.float32, jnp.bfloat16, jnp.int32, jnp.int16
top = 32767.0
split = 768


def kernel(
    g_ref, head_t, lab_ref, cw_ref, fold_in, inv_in,
    fout, pre_ref,
    g_t, t_mid, hall, call, pall, wt, inv, fold, part_x, total_z, part_z, total_x,
    *rest,
):
    moves, rest = [rest[i * 7 : i * 7 + 7] for i in range(4)], rest[28:]
    row, tab1, tabc, tab2, h_send, h_recv, g_send, g_recv, p_send, p_recv, *rest = rest
    t_send, t_recv, w_send, w1_recv, w2_recv, loc = rest
    r, c = lax.axis_index("crow"), lax.axis_index("ccol")
    y, zl, k = r // 4, (r // 2) % 2, r % 2
    zh, x = c // 4, c % 4
    rid = lambda y, zl, k: lax.rem(y + 8, 4) * 4 + zl * 2 + k
    cid = lambda zh, x: lax.rem(zh + 8, 4) * 4 + lax.rem(x + 8, 4)
    y_right, y_left = (rid(y + 1, zl, k), c), (rid(y - 1, zl, k), c)
    pair, sibling = (rid(y, 1 - zl, k), c), (rid(y, zl, 1 - k), c)
    wrap = lambda v: lax.rem(v + 8, 4)
    x_right, x_left = (r, cid(zh, x + 1)), (r, cid(zh, x - 1))
    z_right, z_left = (r, cid(zh + 1, x)), (r, cid(zh - 1, x))

    mine = 2 * zl + k
    pick = lambda odd, a, b: jnp.where(lax.rem(odd, 2) == 1, a, b)
    shift = lambda q, v: pick(v, jnp.where(q < 2, 3 - q, q - 2), jnp.where(q == 0, 0, jnp.where(q == 1, 3, q - 1)))
    unshift = lambda d, v: pick(v, jnp.where(d < 2, d + 2, 3 - d), jnp.where(d == 0, 0, jnp.where(d == 3, 1, d + 1)))
    t1_to = (rid(y, x // 2, lax.rem(x, 2)), cid(zh + shift(mine, x), x + zh + y))
    far = wrap(x - mine - y)
    off = unshift(wrap(zh - far), mine)
    t1_from = (rid(y, off // 2, lax.rem(off, 2)), far * 4 + mine)
    t1_stays = (t1_to[0] == r) & (t1_to[1] == c)
    t2_to = (rid(far, zl, k), c)
    t2_stays = far == y

    barrier = pltpu.get_barrier_semaphore()

    def greet(i, _):
        pl.semaphore_signal(barrier, inc=1, device_id=(lax.rem(r + i, 16), c), device_id_type=MESH)
        pl.semaphore_signal(barrier, inc=1, device_id=(r, lax.rem(c + i, 16)), device_id_type=MESH)
        return 0

    lax.fori_loop(1, 16, greet, 0)

    @pl.when(jnp.logical_not(t1_stays))
    def _():
        pl.semaphore_signal(barrier, inc=1, device_id=t1_to, device_id_type=MESH)
        pl.semaphore_signal(barrier, inc=1, device_id=t1_from, device_id_type=MESH)

    for j in range(8):
        g_t[j * 128 : (j + 1) * 128, :] = g_ref[:, j * 128 : (j + 1) * 128].T
    units = jnp.broadcast_to(cw_ref[...], (8, 64))
    row[:, 0:64] = ((units >> 5) << 5).astype(f32)
    row[:, 64:128] = (units & 31).astype(f32)
    tab1[r] = row[...]

    pl.semaphore_wait(barrier, jnp.where(t1_stays, 30, 32))

    sent = []

    def send(src, dst, ssem, rsem, device):
        copy = pltpu.make_async_remote_copy(
            src_ref=src, dst_ref=dst, send_sem=ssem, recv_sem=rsem, device_id=device, device_id_type=MESH
        )
        copy.start()
        sent.append(copy)

    def landed(dst, rsem):
        pltpu.make_async_copy(dst, dst, rsem).wait()

    quarter = lambda ref, h: ref.at[pl.ds(h * 256, 256)]
    p_half = lambda slot, h: pall.at[slot, pl.ds(h * 512, 512)]

    def step(h, src, dst, ssem, rsem, device):
        return pltpu.make_async_remote_copy(
            src_ref=src, dst_ref=dst, send_sem=ssem, recv_sem=rsem, device_id=device, device_id_type=MESH
        )

    t1 = lambda h: step(h, quarter(g_t, h), quarter(t_mid, h), t_send.at[0], t_recv.at[h], t1_to)
    t2 = lambda h: step(h, quarter(t_mid, h), quarter(pall.at[c], h), t_send.at[1], p_recv.at[c, h // 2], t2_to)

    @pl.when(jnp.logical_not(t1_stays))
    def _():
        for h in range(4):
            t1(h).start()

    @pl.when(t1_stays)
    def _():
        for h in range(4):
            pltpu.make_async_copy(quarter(g_t, h), quarter(t_mid, h), t_recv.at[h]).start()

    def t_pass():
        for h in range(4):
            landed(quarter(t_mid, h), t_recv.at[h])

            @pl.when(jnp.logical_not(t2_stays))
            def _():
                t2(h).start()

            @pl.when(t2_stays)
            def _():
                pltpu.make_async_copy(quarter(t_mid, h), quarter(pall.at[c], h), p_recv.at[c, h // 2]).start()

    class Crow:
        def __init__(self, own, buf, depth, cut, ssem, rsem):
            self.own, self.buf, self.depth, self.cut = own, buf, depth, cut
            self.ssem, self.rsem = ssem, rsem

        def rows(self, h):
            return (0, self.cut) if h == 0 else (self.cut, self.depth - self.cut)

        def at(self, slot, h):
            start, size = self.rows(h)
            return self.buf.at[pl.ds(pl.multiple_of(slot * self.depth + start, 16), size)]

        def push(self, slot, h, device, own=False):
            start, size = self.rows(h)
            src = self.own.at[pl.ds(start, size)] if own else self.at(slot, h)
            send(src, self.at(slot, h), self.ssem, self.rsem.at[slot, h], device)

        def got(self, slot, h):
            landed(self.at(slot, h), self.rsem.at[slot, h])

        def start_pair(self):
            for h in (0, 1):
                self.push(r, h, pair, own=True)

        def start_ring(self):
            for h in (0, 1):
                self.push(r, h, y_right, own=True)
                self.push(r, 1 - h, y_left, own=True)

        def start_sibling(self):
            for h in (0, 1):
                self.push(r, h, sibling, own=True)

        def pass_pair(self):
            slot = rid(y, 1 - zl, k)
            for h in (0, 1):
                self.got(slot, h)
            for h in (0, 1):
                self.push(slot, h, y_right)
                self.push(slot, 1 - h, y_left)
            for h in (0, 1):
                self.push(slot, h, sibling)

        def pass_ring(self, zl):
            a, b = rid(y - 1, zl, k), rid(y + 1, zl, k)
            self.got(a, 0)
            self.push(a, 0, y_right)
            self.got(b, 1)
            self.push(b, 1, y_left)
            self.push(a, 0, sibling)
            self.push(b, 1, sibling)
            self.got(a, 1)
            self.push(a, 1, sibling)
            self.got(b, 0)
            self.push(b, 0, sibling)

        def end_ring(self, zl):
            a = rid(y + 2, zl, k)
            for h in (0, 1):
                self.got(a, h)
                self.push(a, h, sibling)

        def end(self):
            for dy in range(4):
                for z in (0, 1):
                    for h in (0, 1):
                        self.got(rid(y + dy, z, 1 - k), h)
            start = pl.multiple_of(r * self.depth, 16)
            self.buf[pl.ds(start, self.depth), :] = self.own[...]

    heads = Crow(head_t, hall, 80, 48, h_send, h_recv)
    grads = Crow(g_ref, call, 128, 64, g_send, g_recv)

    loads = []
    for d in range(4):
        for zo in range(4):
            owner = zo * 4 + lax.rem(x + d, 4)
            loads.append(
                pltpu.make_async_copy(
                    inv_in.at[pl.ds(pl.multiple_of(owner * 64, 64), 64)],
                    inv.at[d, pl.ds(zo * 64, 64)],
                    loc.at[d],
                )
            )
    fold_load = pltpu.make_async_copy(fold_in, fold, loc.at[4])

    def weights_out(i, _):
        pltpu.make_async_remote_copy(
            src_ref=row, dst_ref=tab1.at[r], send_sem=w_send, recv_sem=w1_recv.at[r],
            device_id=(lax.rem(r + i, 16), c), device_id_type=MESH,
        ).start()
        return 0

    def p_push(slot, h, device):
        send(p_half(slot, h), p_half(slot, h), p_send, p_recv.at[slot, h], device)

    def p_got(slot, h):
        landed(p_half(slot, h), p_recv.at[slot, h])

    def p_start():
        p_got(c, 0)
        p_push(c, 0, z_right)
        p_push(c, 0, x_right)
        p_got(c, 1)
        p_push(c, 1, z_left)
        p_push(c, 1, x_left)
        p_push(c, 1, z_right)
        p_push(c, 0, z_left)
        p_push(c, 1, x_right)
        p_push(c, 0, x_left)

    def z_pass():
        a, b = cid(zh - 1, x), cid(zh + 1, x)
        p_got(a, 0)
        p_push(a, 0, z_right)
        p_got(b, 1)
        p_push(b, 1, z_left)
        p_got(a, 1)
        for h in (0, 1):
            p_push(a, h, x_right)
            p_push(a, 1 - h, x_left)
        p_got(b, 0)
        for h in (0, 1):
            p_push(b, h, x_right)
            p_push(b, 1 - h, x_left)

    def x_pass(dz):
        a, b = cid(zh + dz, x - 1), cid(zh + dz, x + 1)
        p_got(a, 0)
        p_push(a, 0, x_right)
        p_got(b, 1)
        p_push(b, 1, x_left)

    def x_end(dz):
        a, b, o = cid(zh + dz, x - 1), cid(zh + dz, x + 1), cid(zh + dz, x + 2)
        p_got(a, 1)
        p_got(b, 0)
        p_got(o, 0)
        p_got(o, 1)

    def z_end():
        a = cid(zh + 2, x)
        for h in (0, 1):
            p_got(a, h)
            p_push(a, h, x_right)
            p_push(a, h, x_left)

    def dot_heads(left, cols):
        return lax.dot_general(left, hall[cols, :], (((1,), (1,)), ((), ())), preferred_element_type=f32)

    def products_x(d):
        def tile(j, _):
            cols = pl.ds(pl.multiple_of(j * 256, 256), 256)
            part_x[d, :, cols] = dot_heads(inv[d], cols)
            return 0

        lax.fori_loop(0, split // 256, tile, 0)

    def products_z(d):
        rows = pl.ds(pl.multiple_of(lax.rem(zh + d, 4) * 64, 64), 64)
        left = jnp.concatenate([inv[dx, rows, :] for dx in range(4)], axis=0)

        def tile(j, _):
            cols = pl.ds(pl.multiple_of(j * 256, 256), 256)
            part_z[d, :, cols] = dot_heads(left, pl.ds(pl.multiple_of(split + j * 256, 256), 256))
            return 0

        lax.fori_loop(0, (1280 - split) // 256, tile, 0)

    class Reduce:
        def __init__(self, term, left, right, qs, qr, ss, sr, ssem, qsem, usem):
            self.term, self.to = term, (left, right)
            self.qs, self.qr, self.ss, self.sr = qs, qr, ss, sr
            self.ssem, self.qsem, self.usem = ssem, qsem, usem

        def push(self, way, m, value):
            most = jnp.maximum(jnp.max(jnp.abs(value)), 1e-30)
            self.qs[way, m] = jnp.round(value * (top / most)).astype(i32).astype(i16)
            self.ss[way, m] = jnp.full((8, 128), most / top, f32)
            for src, dst, sem in ((self.qs, self.qr, self.qsem), (self.ss, self.sr, self.usem)):
                send(src.at[way, m], dst.at[way, m], self.ssem, sem.at[way, m], self.to[way])

        def pull(self, way, m):
            landed(self.qr.at[way, m], self.qsem.at[way, m])
            landed(self.sr.at[way, m], self.usem.at[way, m])
            unit = self.sr[way, m][0:1, 0:1]
            return self.qr[way, m].astype(i32).astype(f32) * unit

        def first(self):
            self.push(0, 0, self.term(2, 0))
            self.push(1, 0, self.term(2, 1))

        def second(self):
            self.push(0, 1, self.term(3, 1))
            self.push(1, 1, self.term(1, 0))

        def third(self):
            self.push(0, 2, self.term(3, 0) + self.pull(0, 0))
            self.push(1, 2, self.term(1, 1) + self.pull(1, 0))

        def last(self, p):
            own = self.term(0, p)
            return own + self.pull(0, 2 if p == 0 else 1) + self.pull(1, 1 if p == 0 else 2)

        def total(self, ref):
            for p in (0, 1):
                ref[p * 128 : (p + 1) * 128, :] = self.last(p)

        def result(self, cols):
            for p in (0, 1):
                pre_ref[p * 32 : (p + 1) * 32, cols] = self.last(p).astype(bf16)

    def z_term(d, p):
        start = lax.rem(zh + d, 4) * 64 + p * 32
        return total_z[pl.ds(pl.multiple_of(start, 32), 32), :]

    x_first = Reduce(lambda d, p: part_x[d, p * 128 : (p + 1) * 128, :], x_left, x_right, *moves[0])
    then_z = Reduce(z_term, z_left, z_right, *moves[1])
    z_first = Reduce(lambda d, p: part_z[d, p * 128 : (p + 1) * 128, :], z_left, z_right, *moves[2])
    then_x = Reduce(lambda d, p: total_x[d * 64 + p * 32 : d * 64 + p * 32 + 32, :], x_left, x_right, *moves[3])

    def weights_in(i, _):
        slot = lax.rem(r + i, 16)
        landed(tab1.at[slot], w1_recv.at[slot])
        return 0

    def weights_on(i, _):
        pltpu.make_async_remote_copy(
            src_ref=tabc, dst_ref=tab2.at[c], send_sem=w_send, recv_sem=w2_recv.at[c],
            device_id=(r, lax.rem(c + i, 16)), device_id_type=MESH,
        ).start()
        return 0

    def weights_all(i, _):
        slot = lax.rem(c + i, 16)
        landed(tab2.at[slot], w2_recv.at[slot])
        return 0

    heads.start_pair()
    heads.start_ring()
    for load in loads:
        load.start()
    fold_load.start()
    lax.fori_loop(1, 16, weights_out, 0)
    t_pass()
    heads.pass_ring(zl)
    heads.pass_pair()
    heads.start_sibling()
    grads.start_pair()
    p_start()
    heads.pass_ring(1 - zl)
    grads.start_ring()
    heads.end_ring(zl)
    lax.fori_loop(1, 16, weights_in, 0)
    tabc[...] = tab1[:, 0, :].astype(bf16)
    tab2[c] = tabc[...]
    lax.fori_loop(1, 16, weights_on, 0)
    heads.end_ring(1 - zl)
    grads.pass_pair()
    grads.start_sibling()
    heads.end()
    for load in loads:
        load.wait()
    products_x(2)
    x_first.first()
    products_x(3)
    products_x(1)
    x_pass(0)
    products_z(2)
    x_first.second()
    z_first.first()
    grads.pass_ring(zl)
    grads.pass_ring(1 - zl)
    z_pass()
    x_end(0)
    products_z(3)
    x_first.third()
    products_x(0)
    grads.end_ring(1 - zl)
    products_z(1)
    z_first.second()
    products_z(0)
    grads.end_ring(zl)
    x_pass(-1)
    z_first.third()
    z_end()
    grads.end()
    lax.fori_loop(1, 16, weights_all, 0)

    table = tab2[...].reshape(256, 128)
    lanes = lax.broadcasted_iota(i32, (128, 256), 1)
    lane = lax.broadcasted_iota(i32, (128, 128), 1)

    def weigh(b, weight_sum):
        held = wrap(lax.rem(b, 4) - mine - y) * 4 + unshift(wrap(b // 4 - y), mine)
        lab = jnp.broadcast_to(lab_ref[pl.ds(held, 1), :].astype(f32), (128, 128)).T.astype(i32)
        at = ((lab >> 6) & 15) * 16 + (lab >> 10)
        hot = (lanes == jnp.concatenate([at, at], axis=1)).astype(f32).astype(bf16)
        picked = jnp.dot(hot, table, preferred_element_type=f32)
        weight = jnp.sum(jnp.where((lane & 63) == (lab & 63), picked, 0.0), axis=1, keepdims=True) / weight_unit
        rows = pl.ds(pl.multiple_of(held * 128, 128), 128)
        wt[pl.ds(pl.multiple_of(b * 128, 128), 128), :] = (weight * call[rows, :].astype(f32)).astype(bf16)
        return weight_sum + jnp.sum(weight)

    weight_sum = lax.fori_loop(0, 6, weigh, jnp.float32(0.0))
    weight_sum = lax.fori_loop(6, 11, weigh, weight_sum)
    weight_sum = lax.fori_loop(11, 16, weigh, weight_sum)
    gram_unit = (1.0 - stat_decay) / weight_sum
    fold_load.wait()

    def gram(sets, i, j, depth=512):
        value = None
        for dz in sets:
            first = lax.rem(zh + dz + 8, 4) * 4
            left = jnp.concatenate([pall[first + q, pl.ds(i * depth, depth), :] for q in range(4)], axis=1)
            right = wt[pl.ds(pl.multiple_of(first * 128, 512), 512), pl.ds(pl.multiple_of(j * 256, 256), 256)]
            term = jnp.dot(left, right, preferred_element_type=f32)
            value = term if value is None else value + term
        return value

    def gram_early(sets):
        def tile(j, _):
            cols = pl.ds(pl.multiple_of(j * 256, 256), 256)
            for i in range(2):
                rows = pl.ds(i * 512, 512)
                old = fold[rows, cols]
                if sets[0] == 0:
                    old = stat_decay * old
                fold[rows, cols] = old + gram_unit * gram(sets, i, j)
            return 0

        lax.fori_loop(0, 4, tile, 0)

    x_first.total(total_z)
    then_z.first()
    z_first.total(total_x)
    then_x.first()
    x_pass(1)
    then_x.second()
    then_z.second()
    gram_early((0,))
    then_z.third()
    then_x.third()
    x_pass(2)
    x_end(-1)
    gram_early((-1,))
    x_end(1)
    gram_early((1,))
    then_x.result(slice(split, 1280))
    then_z.result(slice(0, split))
    x_end(2)
    stores = []
    for i in range(4):
        rows = pl.ds(i * 256, 256)

        def gram_late(j, _):
            cols = pl.ds(pl.multiple_of(j * 256, 256), 256)
            fold[rows, cols] += gram_unit * gram((2,), i, j, 256)
            return 0

        lax.fori_loop(0, 4, gram_late, 0)
        store = pltpu.make_async_copy(fold.at[rows], fout.at[rows], loc.at[5 + i])
        store.start()
        stores.append(store)

    for copy in sent:
        copy.wait_send()

    @pl.when(jnp.logical_not(t1_stays))
    def _():
        for h in range(4):
            t1(h).wait_send()

    @pl.when(jnp.logical_not(t2_stays))
    def _():
        for h in range(4):
            t2(h).wait_send()

    def weights_left(i, _):
        pltpu.make_async_remote_copy(
            src_ref=row, dst_ref=tab1.at[r], send_sem=w_send, recv_sem=w1_recv.at[r],
            device_id=(lax.rem(r + i, 16), c), device_id_type=MESH,
        ).wait_send()
        pltpu.make_async_remote_copy(
            src_ref=tabc, dst_ref=tab2.at[c], send_sem=w_send, recv_sem=w2_recv.at[c],
            device_id=(r, lax.rem(c + i, 16)), device_id_type=MESH,
        ).wait_send()
        return 0

    lax.fori_loop(1, 16, weights_left, 0)
    for store in stores:
        store.wait()


def messages(rows, columns):
    dma = pltpu.SemaphoreType.DMA
    return (
        *[pltpu.VMEM((2, 3, rows, columns), i16)] * 2,
        *[pltpu.VMEM((2, 3, 8, 128), f32)] * 2,
        dma,
        dma((2, 3)),
        dma((2, 3)),
    )


def body(grad_rows, labels, class_weights, factor_old, inverse_old, head_grad):
    vmem, anywhere = pl.BlockSpec(memory_space=pltpu.VMEM), pl.BlockSpec(memory_space=pl.ANY)
    dma = pltpu.SemaphoreType.DMA
    factor_new, preconditioned = pl.pallas_call(
        kernel,
        out_shape=(
            jax.ShapeDtypeStruct((1024, 1024), f32),
            jax.ShapeDtypeStruct((64, 1280), bf16),
        ),
        in_specs=[vmem, vmem, vmem, vmem, anywhere, anywhere],
        out_specs=(anywhere, vmem),
        scratch_shapes=[
            pltpu.VMEM((1024, 128), bf16),
            pltpu.VMEM((1024, 128), bf16),
            pltpu.VMEM((1280, 1024), bf16),
            pltpu.VMEM((2048, 1024), bf16),
            pltpu.VMEM((16, 1024, 128), bf16),
            pltpu.VMEM((2048, 1024), bf16),
            pltpu.VMEM((4, 256, 1024), bf16),
            pltpu.VMEM((1024, 1024), f32),
            pltpu.VMEM((4, 256, split), f32),
            pltpu.VMEM((256, split), f32),
            pltpu.VMEM((4, 256, 1280 - split), f32),
            pltpu.VMEM((256, 1280 - split), f32),
            *messages(128, split),
            *messages(32, split),
            *messages(128, 1280 - split),
            *messages(32, 1280 - split),
            pltpu.VMEM((8, 128), f32),
            pltpu.VMEM((16, 8, 128), f32),
            pltpu.VMEM((16, 128), bf16),
            pltpu.VMEM((16, 16, 128), bf16),
                dma, dma((16, 2)), dma, dma((16, 2)), dma, dma((16, 2)),
            dma((2,)), dma((4,)), dma, dma((16,)), dma((16,)),
            dma((9,)),
        ],
        compiler_params=pltpu.CompilerParams(
            collective_id=0, has_side_effects=True, vmem_limit_bytes=58 << 20
        ),
        name="kfac",
    )(
        grad_rows,
        head_grad.T,
        labels.reshape(16, 128),
        class_weights.reshape(1, 64),
        factor_old,
        inverse_old,
    )
    return factor_new, preconditioned


def solution(mesh):
    placed = (
        P("crow", "ccol"),
        P(),
        P(("crow", "ccol")),
        P("crow", "ccol"),
        P("crow", "ccol"),
        P("ccol", "crow"),
    )
    return jax.shard_map(
        body,
        mesh=mesh,
        in_specs=placed,
        out_specs=(P("crow", "ccol"), P(("crow", "ccol"), None)),
        check_vma=False,
    )
```
